32 devices in a mesh: parts: 2 (over y), tm: 4 (over z), fiber: 2 (over x), rep: 2 (over core).
Axes of the slice: x: 2, y: 2, z: 4, core: 2. Of those that a mesh axis runs over, the one named last changes fastest.
Arguments:
- strain: bfloat16 [4, 32, 256, 512], P(('parts', 'rep'), None, 'fiber', 'tm'), parts along dimension 0, may hold values from -6 to 6
- time_kernel: bfloat16 [32, 32, 32], replicated, may hold values from -0.1875 to 0.1875
- fiber_kernel: bfloat16 [32, 4, 9], replicated, may hold values from -1 to 1
- cotangent: bfloat16 [4, 32, 2, 128, 256], P(('parts', 'rep'), None, 'fiber', 'tm'), parts along dimension 0, may hold values from -6 to 6
Outputs:
- activation: bfloat16 [4, 32, 2, 128, 256], P(('parts', 'rep'), None, 'fiber', 'tm'), parts along dimension 0
- strain_grad: bfloat16 [4, 32, 256, 512], P(('parts', 'rep'), None, 'fiber', 'tm'), parts along dimension 0
- time_kernel_grad: float32 [64, 32, 32], P('parts'), parts along dimension 0
- fiber_kernel_grad: float32 [64, 4, 9], P('parts'), parts along dimension 0
The draws below stay inside these ranges and needn't reach their ends.
There are 2 independent parts, one for each index of `parts`. The reference program is written for one: setup_inputs(seed, part) draws one part's arguments, and reference() takes and returns one part's arrays. A program takes and returns all parts, laid end to end along the dimension named above; an argument that names none is the same for every part. Nothing has to cross between parts.
All inputs are finite; a program needn't handle non-finite values.
Results may differ from the reference program's by a relative error of at most 0.0095.
Values may be sent and summed in bfloat16 or wider, within the bound.
No kernel may reach another device: no remote copies, remote signals or barrier semaphores. Data moves between devices by JAX's collectives and lax.ppermute only.
A program may use at most 64 MiB of HBM per device.

```python
import math
import jax
import jax.numpy as jnp
from jax import lax

F = 32
GROUPS = 8
KT = 32
KF = 9
CH_DEV = 128
PER = 4
B = 2
FIBERS = 2
CH = 256
T_SIZE = 512
T_OUT = 256


def shard_levels(own_key, dims, pieces, low, largest):
    factor_of, own = 1.0, jax.random.fold_in(own_key, 6)
    for dim, parts in pieces:
        steps = jnp.exp(jax.random.uniform(jax.random.fold_in(own, dim), (parts,), jnp.float32, low / len(pieces), largest / len(pieces)))
        factor_of = factor_of * jnp.repeat(steps, dims[dim] // parts).reshape([-1 if axis == dim else 1 for axis in range(len(dims))])
    return factor_of


def normal_values(stream_key, shape, deviation, reach, shards=(), held_as=jnp.bfloat16):
    values = jax.random.normal(stream_key, shape, jnp.float32) * deviation
    if len(shards) > 0:
        values = shard_levels(stream_key, shape, shards, -0.22, 0.18) * values
    return jnp.clip(values, min=-reach, max=reach).astype(held_as)


def setup_inputs(seed: int = 0, part: int = 0) -> dict:
    key_of = jax.random.split(jax.random.key(seed), 5)
    part_keys = jax.random.split(jax.random.fold_in(key_of[4], part), 5)
    return {
        "strain": normal_values(part_keys[0], (B, F, CH, T_SIZE), 1.0, 6.0, ((0, 2), (2, 2), (3, 4))),
        "time_kernel": normal_values(key_of[1], (F, F, KT), (F * KT) ** -0.5, 0.1875),
        "fiber_kernel": normal_values(key_of[2], (F, PER, KF), (PER * KF) ** -0.5, 1.0),
        "cotangent": normal_values(part_keys[3], (B, F, FIBERS, CH_DEV, T_OUT), 1.0, 6.0, ((0, 2), (2, 2), (3, 4))),
    }


def gelu_slope(value):
    return 0.5 * (1.0 + jax.scipy.special.erf(value / math.sqrt(2.0))) + value * jnp.exp(-0.5 * value * value) / math.sqrt(2.0 * math.pi)

def time_conv(signal, kernel):
    return lax.conv_general_dilated(signal, kernel[:, :, None, :], (1, 2), ((0, 0), (KT - 2, 0)), dimension_numbers=('NCHW', 'OIHW', 'NCHW'), precision=lax.Precision.HIGHEST)

def fiber_conv(signal, kernel):
    return lax.conv_general_dilated(signal, kernel[:, :, :, None], (1, 1), ((KF // 2, KF // 2), (0, 0)), dimension_numbers=('NCHW', 'OIHW', 'NCHW'), feature_group_count=GROUPS, precision=lax.Precision.HIGHEST)

def rounded(value):
    return lax.optimization_barrier(value.astype(jnp.bfloat16)).astype(jnp.float32)

def reference(strain, time_kernel, fiber_kernel, cotangent):
    signal = strain.astype(jnp.float32)
    w_time = time_kernel.astype(jnp.float32)
    w_fiber = fiber_kernel.astype(jnp.float32)
    inner = rounded(time_conv(signal, w_time))
    pre_act = rounded(fiber_conv(inner, w_fiber))
    activation = jax.nn.gelu(pre_act, approximate=False).astype(jnp.bfloat16)
    activation = activation.reshape(B, F, FIBERS, CH_DEV, T_OUT)
    upstream = cotangent.reshape(B, F, CH, T_OUT).astype(jnp.float32)
    d_pre = rounded(upstream * gelu_slope(pre_act))
    unused, back_fiber = jax.vjp(fiber_conv, inner, w_fiber)
    d_inner, g_fiber = back_fiber(d_pre)
    d_inner = rounded(d_inner)
    unused, back_time = jax.vjp(time_conv, signal, w_time)
    d_signal, g_time = back_time(d_inner)
    scale = 1.0 / math.sqrt(B * CH * T_OUT)
    return (activation, d_signal.astype(jnp.bfloat16), g_time * scale, g_fiber * scale)
```

```python
import functools
import math

import jax
import jax.numpy as jnp
from jax import lax
from jax.experimental import pallas as pl
from jax.experimental.pallas import tpu as pltpu
from jax.sharding import PartitionSpec as P

F = 32
PER = 4
TAPS = 32
KF = 9
REACH = KF // 2
CH = 128
STEPS = 128
TOUT = STEPS // 2
HALO = 32
TB = 8
WIN = (2 * TB + TAPS) * F
TG = 4
GROWS = TG * F
NG = TOUT // TG
VWIN = 24 * F
LATE = 16
BF = jnp.bfloat16
F32 = jnp.float32
NT = (((1,), (1,)), ((), ()))
VMEM_LIMIT = 56 * 1024 * 1024


def call(kernel, outs, *args, scratch=(), name=None):
    return pl.pallas_call(
        kernel,
        out_shape=outs,
        in_specs=[pl.BlockSpec(memory_space=pltpu.VMEM)] * len(args),
        out_specs=jax.tree.map(lambda o: pl.BlockSpec(memory_space=pltpu.VMEM), outs),
        scratch_shapes=list(scratch),
        compiler_params=pltpu.CompilerParams(vmem_limit_bytes=VMEM_LIMIT),
        name=name,
    )(*args)


def out(shape, dtype):
    return jax.ShapeDtypeStruct(shape, dtype)


def lanes(shape):
    return lax.broadcasted_iota(jnp.int32, shape, len(shape) - 1)


def rows(shape):
    return lax.broadcasted_iota(jnp.int32, shape, len(shape) - 2)


def roll(x, by, axis=1):
    by = by % x.shape[axis]
    return x if by == 0 else pltpu.roll(x, by, axis)


def pack_kernel(strain_ref, cot_ref, cot_out, halo_out, scratch):
    n = cot_out.shape[0]
    low = lanes((1, 128)) < TOUT
    for f2 in range(F // 2):
        for tile in range(n // 2):
            a = cot_ref[2 * f2, :, 128 * tile : 128 * (tile + 1)].astype(F32)
            b = cot_ref[2 * f2 + 1, :, 128 * tile : 128 * (tile + 1)].astype(F32)
            cot_out[2 * tile, f2] = jnp.where(low, a, roll(b, TOUT)).astype(BF)
            cot_out[2 * tile + 1, f2] = jnp.where(low, roll(a, TOUT), b).astype(BF)
    group = lanes((1, 128)) // HALO
    for i4 in range(F // 4):
        tile = strain_ref[4 * i4].astype(F32)
        tile = roll(tile, HALO)
        for e in range(1, 4):
            other = roll(strain_ref[4 * i4 + e].astype(F32), HALO * (e + 1))
            tile = jnp.where(group == e, other, tile)
        turned = tile.T
        for e in range(4):
            scratch[pl.ds(4 * i4 + e, HALO, stride=F), :] = turned[HALO * e : HALO * (e + 1)]
    halo_out[...] = scratch[...].astype(BF)


def turn_kernel(strain_ref, out_ref, scratch):
    for i in range(F):
        scratch[pl.ds(i, STEPS, stride=F), :] = strain_ref[i].astype(F32).T
    out_ref[...] = scratch[...].astype(BF)


def weight_kernel(wb_ref, vb_ref, d_ref, dt_ref, w_out, v_out, d_out, dt_out):
    base = wb_ref[...].astype(F32)
    base = jnp.concatenate([base, jnp.zeros((F, WIN - base.shape[1]), F32)], axis=1)
    for t in range(TB):
        w_out[F * t : F * (t + 1)] = roll(base, 2 * F * (t + 1)).astype(BF)
    for p in range(2):
        part = vb_ref[F * p : F * (p + 1)].astype(F32)
        part = jnp.concatenate([part, jnp.zeros((F, VWIN - part.shape[1]), F32)], axis=1)
        for h in range(TB):
            v_out[F * (2 * h + p) : F * (2 * h + p + 1)] = roll(part, F * h).astype(BF)
    step = (lanes((1, KF * GROWS)) % GROWS) // F
    for t in range(TG):
        d_out[F * t : F * (t + 1)] = jnp.where(step == t, d_ref[...].astype(F32), 0.0).astype(BF)
        dt_out[F * t : F * (t + 1)] = jnp.where(step == t, dt_ref[...].astype(F32), 0.0).astype(BF)


def pack_edges(read):
    group = lanes((1, 128)) // 8
    packed = jnp.zeros((GROWS, CH), F32)
    for g in range(NG):
        packed = jnp.where(group == g, roll(read(g), 8 * g + REACH), packed)
    return packed.astype(BF)


def edges_of(before_ref, after_ref):
    me, size = lax.axis_index("fiber"), lax.axis_size("fiber")
    first = lanes((1, 128)) % 8 < REACH
    keep_before = jnp.where(me > 0, 1.0, 0.0).astype(F32)
    keep_after = jnp.where(me < size - 1, 1.0, 0.0).astype(F32)
    return jnp.where(first, before_ref[...].astype(F32) * keep_before, after_ref[...].astype(F32) * keep_after)


def shifted_stack(tile, edges, g, shifts):
    around = roll(edges, -(8 * g + REACH))
    lane = lanes((1, 128))
    pieces = []
    for by in shifts:
        if by > 0:
            piece = roll(jnp.where(lane < by, around, tile), -by)
        elif by < 0:
            piece = roll(jnp.where(lane >= CH + by, around, tile), -by)
        else:
            piece = tile
        pieces.append(piece.astype(BF))
    return jnp.concatenate(pieces, axis=0)


def window(early_ref, main_ref, b, size):
    start = 2 * TB * F * b
    early = early_ref.shape[0]
    if start >= early:
        return main_ref[start - early : start - early + size]
    return jnp.concatenate([early_ref[start:early], main_ref[0 : size - (early - start)]], axis=0)


def inner_kernel(halo_ref, strain_ref, w_ref, u_out, edge_out, scratch):
    size = TB * F
    for b in range(0, TOUT // TB, 2):
        pair = jnp.concatenate([window(halo_ref, strain_ref, b + k, WIN) for k in range(2)], axis=1)
        u = jnp.dot(w_ref[...], pair, preferred_element_type=F32)
        for k in range(2):
            scratch[size * (b + k) : size * (b + k + 1)] = u[:, CH * k : CH * (k + 1)]
            u_out[size * (b + k) : size * (b + k + 1)] = u[:, CH * k : CH * (k + 1)].astype(BF)
    edge_out[...] = pack_edges(lambda g: scratch[GROWS * g : GROWS * (g + 1)])


def forward_kernel(u_ref, before_ref, after_ref, d_ref, act_out, slope_out, scratch):
    edges = edges_of(before_ref, after_ref)
    for g in range(0, NG, 2):
        pair = jnp.concatenate(
            [
                shifted_stack(
                    u_ref[GROWS * (g + k) : GROWS * (g + k + 1)].astype(F32), edges, g + k, range(-REACH, REACH + 1)
                )
                for k in range(2)
            ],
            axis=1,
        )
        z = jnp.dot(d_ref[...], pair, preferred_element_type=F32).astype(BF).astype(F32)
        half = 0.5 * (1.0 + lax.erf(z * (1.0 / math.sqrt(2.0))))
        slope = half + z * jnp.exp(-0.5 * z * z) * (1.0 / math.sqrt(2.0 * math.pi))
        act = z * half
        for k in range(2):
            where = slice(GROWS * (g + k), GROWS * (g + k + 1))
            scratch[where] = act[:, CH * k : CH * (k + 1)]
            slope_out[where] = slope[:, CH * k : CH * (k + 1)]
    n, _, local, _ = act_out.shape
    for f2 in range(F // 2):
        both = jnp.concatenate([scratch[pl.ds(2 * f2 + e, TOUT, stride=F), :] for e in range(2)], axis=0)
        turned = both.T
        for q in range(n):
            act_out[q, f2] = turned[local * q : local * (q + 1)].astype(BF)


def slope_kernel(slope_ref, cot_ref, dz_out, edge_out, scratch):
    n, _, local, _ = cot_ref.shape
    for f2 in range(F // 2):
        turned = cot_ref[:, f2].astype(F32).reshape(CH, 128).T
        for e in range(2):
            scratch[pl.ds(2 * f2 + e, TOUT, stride=F), :] = turned[TOUT * e : TOUT * (e + 1)]
    dz = (scratch[...] * slope_ref[...]).astype(BF)
    dz_out[...] = dz
    scratch[...] = dz.astype(F32)
    edge_out[...] = pack_edges(lambda g: scratch[GROWS * g : GROWS * (g + 1)])


def backward_kernel(dz_ref, before_ref, after_ref, dt_ref, u_ref, halo_ref, strain_ref, du_out, grad_out):
    edges = edges_of(before_ref, after_ref)
    taps = jnp.zeros((GROWS, KF * GROWS), F32)
    for g in range(0, NG, 2):
        stacks = [
            shifted_stack(
                dz_ref[GROWS * (g + k) : GROWS * (g + k + 1)].astype(F32),
                edges,
                g + k,
                [REACH - m for m in range(KF)],
            )
            for k in range(2)
        ]
        pair = jnp.concatenate(stacks, axis=1)
        du = jnp.dot(dt_ref[...], pair, preferred_element_type=F32).astype(BF)
        u = jnp.concatenate([u_ref[GROWS * (g + k) : GROWS * (g + k + 1)] for k in range(2)], axis=1)
        taps = taps + lax.dot_general(u, pair, NT, preferred_element_type=F32)
        for k in range(2):
            du_out[GROWS * (g + k) : GROWS * (g + k + 1)] = du[:, CH * k : CH * (k + 1)]
    lane = lanes((1, KF * GROWS))
    step = (lane % GROWS) // F
    kept = jnp.where(step == 0, taps[0:F], 0.0)
    for t in range(1, TG):
        kept = jnp.where(step == t, taps[F * t : F * (t + 1)], kept)
    feat = lane % F
    row = rows((F, 1))
    lines = []
    for j in range(PER):
        lines.append(jnp.sum(jnp.where(row == feat // PER * PER + j, kept, 0.0), axis=0, keepdims=True))
    lines = jnp.concatenate(lines + [jnp.zeros((8 - PER, KF * GROWS), F32)], axis=0)
    tiles = []
    for top in range(0, KF, TG):
        tile = jnp.zeros((8, GROWS), F32)
        for m in range(top, min(KF, top + TG)):
            line = lines[:, GROWS * m : GROWS * (m + 1)]
            total = line
            for t in range(1, TG):
                total = total + roll(line, F * t)
            tile = jnp.where(lanes((1, GROWS)) // F == m - top, total, tile)
        tiles.append(tile)
    size = TB * F
    wide = jnp.zeros((size, WIN), F32)
    for b in range(0, TOUT // TB, 2):
        left = jnp.concatenate([du_out[size * (b + k) : size * (b + k + 1)] for k in range(2)], axis=1)
        right = jnp.concatenate([window(halo_ref, strain_ref, b + k, WIN) for k in range(2)], axis=1)
        wide = wide + lax.dot_general(left, right, NT, preferred_element_type=F32)
    total = jnp.zeros((F, WIN), F32)
    for t in range(TB):
        total = total + roll(wide[F * t : F * (t + 1)], -2 * F * (t + 1))
    grad_out[0:F] = total[:, 0 : TAPS * F]
    tiles.append(jnp.zeros((8, TAPS * F - len(tiles) * GROWS), F32))
    grad_out[F : F + 8] = jnp.concatenate(tiles, axis=1)


def signal_kernel(du_ref, late_ref, v_ref, grad_out, scratch):
    size = TB * F
    last = TOUT * F

    def rows_of(b):
        start, stop = size * b, size * b + VWIN
        if stop <= last:
            return du_ref[start:stop]
        return jnp.concatenate([du_ref[start:last], late_ref[0 : stop - last]], axis=0)

    step = 2 * TB * F
    for b in range(0, TOUT // TB, 2):
        pair = jnp.concatenate([rows_of(b + k) for k in range(2)], axis=1)
        part = jnp.dot(v_ref[...], pair, preferred_element_type=F32)
        for k in range(2):
            scratch[step * (b + k) : step * (b + k + 1)] = part[:, CH * k : CH * (k + 1)]
    for i in range(F):
        grad_out[i] = scratch[pl.ds(i, STEPS, stride=F), :].T.astype(BF)


def unpack_kernel(act_ref, act_out):
    n = act_ref.shape[0]
    low = lanes((1, 128)) < TOUT
    for f2 in range(F // 2):
        for tile in range(n // 2):
            a = act_ref[2 * tile, f2].astype(F32)
            b = act_ref[2 * tile + 1, f2].astype(F32)
            where = slice(128 * tile, 128 * (tile + 1))
            act_out[2 * f2, :, where] = jnp.where(low, a, roll(b, TOUT)).astype(BF)
            act_out[2 * f2 + 1, :, where] = jnp.where(low, roll(a, TOUT), b).astype(BF)


def neighbours(array, axis):
    size = lax.axis_size(axis)
    if size == 2:
        other = lax.ppermute(array, axis, [(0, 1), (1, 0)])
        return other, other
    before = lax.ppermute(array, axis, [(i, i + 1) for i in range(size - 1)])
    after = lax.ppermute(array, axis, [(i + 1, i) for i in range(size - 1)])
    return before, after


def summed(array, axes):
    for axis in axes:
        size = lax.axis_size(axis)
        hop = 1
        while hop < size:
            mine = array.astype(BF)
            other = lax.ppermute(mine, axis, [(i, i ^ hop) for i in range(size)])
            array = mine.astype(F32) + other.astype(F32)
            hop *= 2
    return array


def on_device(strain, time_kernel, fiber_kernel, cotangent):
    n = lax.axis_size("tm")
    size = lax.axis_size("rep") * CH * lax.axis_size("fiber") * TOUT * n
    scale = 1.0 / math.sqrt(size)
    local = cotangent.shape[3]
    x = strain[0]
    packed = (n, F // 2, local, 128)
    sent, tail = call(
        pack_kernel,
        (out(packed, BF), out((HALO * F, CH), BF)),
        x,
        cotangent[0, :, 0],
        scratch=[pltpu.VMEM((HALO * F, CH), F32)],
        name="pack",
    )
    upstream = lax.all_to_all(sent, "tm", 0, 0, tiled=True)
    halo = lax.ppermute(tail, "tm", [(i, i + 1) for i in range(n - 1)])

    wb = jnp.transpose(time_kernel, (0, 2, 1)).reshape(F, TAPS * F)
    vb = time_kernel.reshape(F, F, TAPS // 2, 2)[:, :, ::-1]
    vb = jnp.transpose(vb, (3, 1, 2, 0)).reshape(2 * F, TAPS // 2 * F)
    ids = jnp.arange(F, dtype=jnp.int32) // PER
    same = ids[:, None] == ids[None, :]
    dense = jnp.where(same[:, :, None], jnp.tile(fiber_kernel, (1, F // PER, 1)), jnp.zeros((), BF))
    d0 = jnp.tile(jnp.transpose(dense, (0, 2, 1)), (1, 1, TG)).reshape(F, KF * GROWS)
    dt0 = jnp.tile(jnp.transpose(dense, (1, 2, 0)), (1, 1, TG)).reshape(F, KF * GROWS)
    w, v, d, dt = call(
        weight_kernel,
        (
            out((TB * F, WIN), BF),
            out((2 * TB * F, VWIN), BF),
            out((GROWS, KF * GROWS), BF),
            out((GROWS, KF * GROWS), BF),
        ),
        wb,
        vb,
        d0,
        dt0,
        name="weights",
    )
    (turned,) = call(
        turn_kernel, (out((STEPS * F, CH), BF),), x, scratch=[pltpu.VMEM((STEPS * F, CH), F32)], name="turn"
    )
    flat = (TOUT * F, CH)
    u, u_edge = call(
        inner_kernel,
        (out(flat, BF), out((GROWS, CH), BF)),
        halo,
        turned,
        w,
        scratch=[pltpu.VMEM(flat, F32)],
        name="inner",
    )
    before, after = neighbours(u_edge, "fiber")
    act, slope = call(
        forward_kernel,
        (out(packed, BF), out(flat, F32)),
        u,
        before,
        after,
        d,
        scratch=[pltpu.VMEM(flat, F32)],
        name="forward",
    )
    act = lax.all_to_all(act, "tm", 0, 0, tiled=True)
    dz, dz_edge = call(
        slope_kernel,
        (out(flat, BF), out((GROWS, CH), BF)),
        slope,
        upstream,
        scratch=[pltpu.VMEM(flat, F32)],
        name="slope",
    )
    before, after = neighbours(dz_edge, "fiber")
    du, grads = call(
        backward_kernel,
        (out(flat, BF), out((F + 8, TAPS * F), F32)),
        dz,
        before,
        after,
        dt,
        u,
        halo,
        turned,
        name="backward",
    )
    late = lax.ppermute(du[0 : LATE * F], "tm", [(i + 1, i) for i in range(n - 1)])
    grads = summed(grads, ("rep", "fiber", "tm")) * scale
    (strain_grad,) = call(
        signal_kernel,
        (out((F, CH, STEPS), BF),),
        du,
        late,
        v,
        scratch=[pltpu.VMEM((STEPS * F, CH), F32)],
        name="signal",
    )
    (activation,) = call(unpack_kernel, (out((F, local, n * TOUT), BF),), act, name="unpack")
    time_grad = jnp.transpose(grads[0:F].reshape(F, TAPS, F), (0, 2, 1))
    fiber_grad = grads[F : F + PER, 0 : KF * F].reshape(PER, KF, F)
    fiber_grad = jnp.transpose(fiber_grad, (2, 0, 1))
    return activation[None, :, None], strain_grad[None], time_grad, fiber_grad


def solution(mesh):
    placed = (
        P(("parts", "rep"), None, "fiber", "tm"),
        P(),
        P(),
        P(("parts", "rep"), None, "fiber", "tm", None),
    )
    return jax.shard_map(
        on_device,
        mesh=mesh,
        in_specs=placed,
        out_specs=(
            P(("parts", "rep"), None, "fiber", "tm", None),
            P(("parts", "rep"), None, "fiber", "tm"),
            P("parts", None, None),
            P("parts", None, None),
        ),
        check_vma=False,
    )
```

```python
import functools
import math

import jax
import jax.numpy as jnp
from jax import lax
from jax.experimental import pallas as pl
from jax.experimental.pallas import tpu as pltpu
from jax.sharding import PartitionSpec as P

F = 32
PER = 4
TAPS = 32
KF = 9
REACH = KF // 2
CH = 128
STEPS = 128
TOUT = STEPS // 2
HALO = 32
TB = 8
WIN = (2 * TB + TAPS) * F
TG = 4
GROWS = TG * F
NG = TOUT // TG
VWIN = 24 * F
LATE = 16
BF = jnp.bfloat16
F32 = jnp.float32
NT = (((1,), (1,)), ((), ()))
VMEM_LIMIT = 16 * 1024 * 1024


def call(kernel, outs, *args, scratch=(), name=None):
    return pl.pallas_call(
        kernel,
        out_shape=outs,
        in_specs=[pl.BlockSpec(memory_space=pltpu.VMEM)] * len(args),
        out_specs=jax.tree.map(lambda o: pl.BlockSpec(memory_space=pltpu.VMEM), outs),
        scratch_shapes=list(scratch),
        compiler_params=pltpu.CompilerParams(vmem_limit_bytes=VMEM_LIMIT),
        name=name,
    )(*args)


def out(shape, dtype):
    return jax.ShapeDtypeStruct(shape, dtype)


def lanes(shape):
    return lax.broadcasted_iota(jnp.int32, shape, len(shape) - 1)


def rows(shape):
    return lax.broadcasted_iota(jnp.int32, shape, len(shape) - 2)


def roll(x, by, axis=1):
    by = by % x.shape[axis]
    return x if by == 0 else pltpu.roll(x, by, axis)


def place(chunks, refs):
    me = lax.axis_index("tm")
    for hop, ref in enumerate(refs):
        ref[...] = chunks[me ^ hop]


def gather(chunks, refs):
    me = lax.axis_index("tm")
    for hop, ref in enumerate(refs):
        chunks[me ^ hop] = ref[...]


def pack_kernel(cot_ref, *refs):
    chunks = refs[-1]
    n = chunks.shape[0]
    low = lanes((1, 128)) < TOUT
    for f2 in range(F // 2):
        for tile in range(n // 2):
            a = cot_ref[2 * f2, :, 128 * tile : 128 * (tile + 1)]
            b = cot_ref[2 * f2 + 1, :, 128 * tile : 128 * (tile + 1)]
            chunks[2 * tile, f2] = jnp.where(low, a, roll(b, TOUT))
            chunks[2 * tile + 1, f2] = jnp.where(low, roll(a, TOUT), b)
    place(chunks, refs[:-1])


def tail_kernel(strain_ref, halo_out, scratch):
    group = lanes((1, 128)) // HALO
    for i4 in range(F // 4):
        tile = roll(strain_ref[4 * i4], HALO)
        for e in range(1, 4):
            tile = jnp.where(group == e, roll(strain_ref[4 * i4 + e], HALO * (e + 1)), tile)
        turned = tile.T.astype(F32)
        for e in range(4):
            scratch[pl.ds(4 * i4 + e, HALO, stride=F), :] = turned[HALO * e : HALO * (e + 1)]
    halo_out[...] = scratch[...].astype(BF)


def turn_kernel(strain_ref, out_ref, scratch):
    for i in range(F):
        scratch[pl.ds(i, STEPS, stride=F), :] = strain_ref[i].T.astype(F32)
    out_ref[...] = scratch[...].astype(BF)


def weight_kernel(wb_ref, vb_ref, d_ref, dt_ref, w_out, v_out, d_out, dt_out):
    base = wb_ref[...].astype(F32)
    base = jnp.concatenate([base, jnp.zeros((F, WIN - base.shape[1]), F32)], axis=1)
    for t in range(TB):
        w_out[F * t : F * (t + 1)] = roll(base, 2 * F * (t + 1)).astype(BF)
    for p in range(2):
        part = vb_ref[F * p : F * (p + 1)].astype(F32)
        part = jnp.concatenate([part, jnp.zeros((F, VWIN - part.shape[1]), F32)], axis=1)
        for h in range(TB):
            v_out[F * (2 * h + p) : F * (2 * h + p + 1)] = roll(part, F * h).astype(BF)
    step = (lanes((1, KF * GROWS)) % GROWS) // F
    for t in range(TG):
        d_out[F * t : F * (t + 1)] = jnp.where(step == t, d_ref[...].astype(F32), 0.0).astype(BF)
        dt_out[F * t : F * (t + 1)] = jnp.where(step == t, dt_ref[...].astype(F32), 0.0).astype(BF)


def pack_edges(read):
    group = lanes((1, 128)) // 8
    packed = roll(read(0), REACH)
    for g in range(1, NG):
        packed = jnp.where(group == g, roll(read(g), 8 * g + REACH), packed)
    return packed


def edges_of(before_ref, after_ref):
    me, size = lax.axis_index("fiber"), lax.axis_size("fiber")
    first = lanes((1, 128)) % 8 < REACH
    keep_before = jnp.where(me > 0, 1.0, 0.0).astype(F32)
    keep_after = jnp.where(me < size - 1, 1.0, 0.0).astype(F32)
    both = jnp.where(first, before_ref[...].astype(F32) * keep_before, after_ref[...].astype(F32) * keep_after)
    return both.astype(BF)


def shifted_stack(tile, edges, g, shifts):
    around = roll(edges, -(8 * g + REACH))
    lane = lanes((1, 128))
    pieces = []
    for by in shifts:
        if by > 0:
            pieces.append(roll(jnp.where(lane < by, around, tile), -by))
        elif by < 0:
            pieces.append(roll(jnp.where(lane >= CH + by, around, tile), -by))
        else:
            pieces.append(tile)
    return jnp.concatenate(pieces, axis=0)


def window(early_ref, main_ref, b, size):
    start = 2 * TB * F * b
    early = early_ref.shape[0]
    if start >= early:
        return main_ref[start - early : start - early + size]
    return jnp.concatenate([early_ref[start:early], main_ref[0 : size - (early - start)]], axis=0)


def inner_kernel(halo_ref, strain_ref, w_ref, u_out, edge_out):
    size = TB * F
    for b in range(0, TOUT // TB, 2):
        pair = jnp.concatenate([window(halo_ref, strain_ref, b + k, WIN) for k in range(2)], axis=1)
        u = jnp.dot(w_ref[...], pair, preferred_element_type=F32)
        for k in range(2):
            u_out[size * (b + k) : size * (b + k + 1)] = u[:, CH * k : CH * (k + 1)].astype(BF)
    edge_out[...] = pack_edges(lambda g: u_out[GROWS * g : GROWS * (g + 1)])


def forward_kernel(u_ref, before_ref, after_ref, d_ref, slope_out, *refs):
    chunks, scratch = refs[-2:]
    edges = edges_of(before_ref, after_ref)
    for g in range(0, NG, 2):
        pair = jnp.concatenate(
            [
                shifted_stack(
                    u_ref[GROWS * (g + k) : GROWS * (g + k + 1)], edges, g + k, range(-REACH, REACH + 1)
                )
                for k in range(2)
            ],
            axis=1,
        )
        z = jnp.dot(d_ref[...], pair, preferred_element_type=F32).astype(BF).astype(F32)
        half = 0.5 * (1.0 + lax.erf(z * (1.0 / math.sqrt(2.0))))
        slope = half + z * jnp.exp(-0.5 * z * z) * (1.0 / math.sqrt(2.0 * math.pi))
        act = z * half
        for k in range(2):
            where = slice(GROWS * (g + k), GROWS * (g + k + 1))
            scratch[where] = act[:, CH * k : CH * (k + 1)]
            slope_out[where] = slope[:, CH * k : CH * (k + 1)]
    n, _, local, _ = chunks.shape
    for f2 in range(F // 2):
        both = jnp.concatenate([scratch[pl.ds(2 * f2 + e, TOUT, stride=F), :] for e in range(2)], axis=0)
        turned = both.T
        for q in range(n):
            chunks[q, f2] = turned[local * q : local * (q + 1)].astype(BF)
    place(chunks, refs[:-2])


def slope_kernel(slope_ref, *refs):
    dz_out, edge_out, chunks, scratch = refs[-4:]
    gather(chunks, refs[:-4])
    local = chunks.shape[2]
    for f2 in range(F // 2):
        if local % 16 == 0:
            turned = chunks[:, f2].reshape(CH, 128).T.astype(F32)
        else:
            turned = chunks[:, f2].astype(F32).reshape(CH, 128).T
        for e in range(2):
            scratch[pl.ds(2 * f2 + e, TOUT, stride=F), :] = turned[TOUT * e : TOUT * (e + 1)]
    dz_out[...] = (scratch[...] * slope_ref[...]).astype(BF)
    edge_out[...] = pack_edges(lambda g: dz_out[GROWS * g : GROWS * (g + 1)])


def backward_kernel(dz_ref, before_ref, after_ref, dt_ref, u_ref, halo_ref, strain_ref, du_out, grad_out):
    edges = edges_of(before_ref, after_ref)
    taps = jnp.zeros((GROWS, KF * GROWS), F32)
    for g in range(0, NG, 2):
        stacks = [
            shifted_stack(
                dz_ref[GROWS * (g + k) : GROWS * (g + k + 1)],
                edges,
                g + k,
                [REACH - m for m in range(KF)],
            )
            for k in range(2)
        ]
        pair = jnp.concatenate(stacks, axis=1)
        du = jnp.dot(dt_ref[...], pair, preferred_element_type=F32).astype(BF)
        u = jnp.concatenate([u_ref[GROWS * (g + k) : GROWS * (g + k + 1)] for k in range(2)], axis=1)
        taps = taps + lax.dot_general(u, pair, NT, preferred_element_type=F32)
        for k in range(2):
            du_out[GROWS * (g + k) : GROWS * (g + k + 1)] = du[:, CH * k : CH * (k + 1)]
    lane = lanes((1, KF * GROWS))
    step = (lane % GROWS) // F
    kept = jnp.where(step == 0, taps[0:F], 0.0)
    for t in range(1, TG):
        kept = jnp.where(step == t, taps[F * t : F * (t + 1)], kept)
    feat = lane % F
    row = rows((F, 1))
    lines = []
    for j in range(PER):
        lines.append(jnp.sum(jnp.where(row == feat // PER * PER + j, kept, 0.0), axis=0, keepdims=True))
    lines = jnp.concatenate(lines + [jnp.zeros((8 - PER, KF * GROWS), F32)], axis=0)
    tiles = []
    for top in range(0, KF, TG):
        tile = jnp.zeros((8, GROWS), F32)
        for m in range(top, min(KF, top + TG)):
            line = lines[:, GROWS * m : GROWS * (m + 1)]
            total = line
            for t in range(1, TG):
                total = total + roll(line, F * t)
            tile = jnp.where(lanes((1, GROWS)) // F == m - top, total, tile)
        tiles.append(tile)
    size = TB * F
    wide = jnp.zeros((size, WIN), F32)
    for b in range(0, TOUT // TB, 2):
        left = jnp.concatenate([du_out[size * (b + k) : size * (b + k + 1)] for k in range(2)], axis=1)
        right = jnp.concatenate([window(halo_ref, strain_ref, b + k, WIN) for k in range(2)], axis=1)
        wide = wide + lax.dot_general(left, right, NT, preferred_element_type=F32)
    total = jnp.zeros((F, WIN), F32)
    for t in range(TB):
        total = total + roll(wide[F * t : F * (t + 1)], -2 * F * (t + 1))
    grad_out[0:F] = total[:, 0 : TAPS * F]
    tiles.append(jnp.zeros((8, TAPS * F - len(tiles) * GROWS), F32))
    grad_out[F : F + 8] = jnp.concatenate(tiles, axis=1)


def signal_kernel(du_ref, late_ref, v_ref, grad_out, scratch):
    size = TB * F
    last = TOUT * F

    def rows_of(b):
        start, stop = size * b, size * b + VWIN
        if stop <= last:
            return du_ref[start:stop]
        return jnp.concatenate([du_ref[start:last], late_ref[0 : stop - last]], axis=0)

    step = 2 * TB * F
    for b in range(0, TOUT // TB, 2):
        pair = jnp.concatenate([rows_of(b + k) for k in range(2)], axis=1)
        part = jnp.dot(v_ref[...], pair, preferred_element_type=F32)
        for k in range(2):
            scratch[step * (b + k) : step * (b + k + 1)] = part[:, CH * k : CH * (k + 1)]
    for i in range(F):
        grad_out[i] = scratch[pl.ds(i, STEPS, stride=F), :].astype(BF).T


def unpack_kernel(*refs):
    act_out, chunks = refs[-2:]
    gather(chunks, refs[:-2])
    n = chunks.shape[0]
    low = lanes((1, 128)) < TOUT
    for f2 in range(F // 2):
        for tile in range(n // 2):
            a = chunks[2 * tile, f2]
            b = chunks[2 * tile + 1, f2]
            where = slice(128 * tile, 128 * (tile + 1))
            act_out[2 * f2, :, where] = jnp.where(low, a, roll(b, TOUT))
            act_out[2 * f2 + 1, :, where] = jnp.where(low, roll(a, TOUT), b)


def exchanged(chunks):
    size = len(chunks)
    got = [chunks[0]]
    for hop in range(1, size):
        got.append(lax.ppermute(chunks[hop], "tm", [(i, i ^ hop) for i in range(size)]))
    return got


def neighbours(array, axis):
    size = lax.axis_size(axis)
    if size == 2:
        other = lax.ppermute(array, axis, [(0, 1), (1, 0)])
        return other, other
    before = lax.ppermute(array, axis, [(i, i + 1) for i in range(size - 1)])
    after = lax.ppermute(array, axis, [(i + 1, i) for i in range(size - 1)])
    return before, after


def summed(array, axes):
    for axis in axes:
        size = lax.axis_size(axis)
        hop = 1
        while hop < size:
            mine = array.astype(BF)
            other = lax.ppermute(mine, axis, [(i, i ^ hop) for i in range(size)])
            array = mine.astype(F32) + other.astype(F32)
            hop *= 2
    return array


def on_device(strain, time_kernel, fiber_kernel, cotangent):
    n = lax.axis_size("tm")
    size = lax.axis_size("rep") * CH * lax.axis_size("fiber") * TOUT * n
    scale = 1.0 / math.sqrt(size)
    local = cotangent.shape[3]
    x = strain[0]
    chunk = (F // 2, local, 128)
    packed = (n,) + chunk
    flat = (TOUT * F, CH)
    (tail,) = call(
        tail_kernel, (out((HALO * F, CH), BF),), x, scratch=[pltpu.VMEM((HALO * F, CH), F32)], name="tail"
    )
    halo = lax.ppermute(tail, "tm", [(i, i + 1) for i in range(n - 1)])
    cot, tail = lax.optimization_barrier((cotangent[0, :, 0], tail))
    sent = call(pack_kernel, (out(chunk, BF),) * n, cot, scratch=[pltpu.VMEM(packed, BF)], name="pack")
    upstream = exchanged(sent)

    wb = jnp.transpose(time_kernel, (0, 2, 1)).reshape(F, TAPS * F)
    vb = time_kernel.reshape(F, F, TAPS // 2, 2)[:, :, ::-1]
    vb = jnp.transpose(vb, (3, 1, 2, 0)).reshape(2 * F, TAPS // 2 * F)
    ids = jnp.arange(F, dtype=jnp.int32) // PER
    same = ids[:, None] == ids[None, :]
    dense = jnp.where(same[:, :, None], jnp.tile(fiber_kernel, (1, F // PER, 1)), jnp.zeros((), BF))
    d0 = jnp.tile(jnp.transpose(dense, (0, 2, 1)), (1, 1, TG)).reshape(F, KF * GROWS)
    dt0 = jnp.tile(jnp.transpose(dense, (1, 2, 0)), (1, 1, TG)).reshape(F, KF * GROWS)
    w, v, d, dt = call(
        weight_kernel,
        (
            out((TB * F, WIN), BF),
            out((2 * TB * F, VWIN), BF),
            out((GROWS, KF * GROWS), BF),
            out((GROWS, KF * GROWS), BF),
        ),
        wb,
        vb,
        d0,
        dt0,
        name="weights",
    )
    (turned,) = call(
        turn_kernel, (out((STEPS * F, CH), BF),), x, scratch=[pltpu.VMEM((STEPS * F, CH), F32)], name="turn"
    )
    u, u_edge = call(
        inner_kernel,
        (out(flat, BF), out((GROWS, CH), BF)),
        halo,
        turned,
        w,
        name="inner",
    )
    before, after = neighbours(u_edge, "fiber")
    slope, *act = call(
        forward_kernel,
        (out(flat, F32),) + (out(chunk, BF),) * n,
        u,
        before,
        after,
        d,
        scratch=[pltpu.VMEM(packed, BF), pltpu.VMEM(flat, F32)],
        name="forward",
    )
    act = exchanged(act)
    dz, dz_edge = call(
        slope_kernel,
        (out(flat, BF), out((GROWS, CH), BF)),
        slope,
        *upstream,
        scratch=[pltpu.VMEM(packed, BF), pltpu.VMEM(flat, F32)],
        name="slope",
    )
    before, after = neighbours(dz_edge, "fiber")
    du, grads = call(
        backward_kernel,
        (out(flat, BF), out((F + 8, TAPS * F), F32)),
        dz,
        before,
        after,
        dt,
        u,
        halo,
        turned,
        name="backward",
    )
    late = lax.ppermute(du[0 : LATE * F], "tm", [(i + 1, i) for i in range(n - 1)])
    grads = summed(grads, ("rep", "fiber", "tm")) * scale
    (strain_grad,) = call(
        signal_kernel,
        (out((F, CH, STEPS), BF),),
        du,
        late,
        v,
        scratch=[pltpu.VMEM((STEPS * F, CH), F32)],
        name="signal",
    )
    (activation,) = call(
        unpack_kernel, (out((F, local, n * TOUT), BF),), *act, scratch=[pltpu.VMEM(packed, BF)], name="unpack"
    )
    time_grad = jnp.transpose(grads[0:F].reshape(F, TAPS, F), (0, 2, 1))
    fiber_grad = grads[F : F + PER, 0 : KF * F].reshape(PER, KF, F)
    fiber_grad = jnp.transpose(fiber_grad, (2, 0, 1))
    return activation[None, :, None], strain_grad[None], time_grad, fiber_grad


def solution(mesh):
    placed = (
        P(("parts", "rep"), None, "fiber", "tm"),
        P(),
        P(),
        P(("parts", "rep"), None, "fiber", "tm", None),
    )
    return jax.shard_map(
        on_device,
        mesh=mesh,
        in_specs=placed,
        out_specs=(
            P(("parts", "rep"), None, "fiber", "tm", None),
            P(("parts", "rep"), None, "fiber", "tm"),
            P("parts", None, None),
            P("parts", None, None),
        ),
        check_vma=False,
    )
```

```python
import functools
import math

import jax
import jax.numpy as jnp
from jax import lax
from jax.experimental import pallas as pl
from jax.experimental.pallas import tpu as pltpu
from jax.sharding import PartitionSpec as P

F = 32
PER = 4
TAPS = 32
KF = 9
REACH = KF // 2
CH = 128
STEPS = 128
TOUT = STEPS // 2
HALO = 32
TB = 8
WIN = (2 * TB + TAPS) * F
TG = 4
GROWS = TG * F
NG = TOUT // TG
VWIN = 24 * F
LATE = 16
BF = jnp.bfloat16
F32 = jnp.float32
NT = (((1,), (1,)), ((), ()))
VMEM_LIMIT = 16 * 1024 * 1024


def call(kernel, outs, *args, scratch=(), name=None, far=(), far_outs=()):
    where = lambda k, away: pl.BlockSpec(memory_space=pltpu.HBM if k in away else pltpu.VMEM)
    return pl.pallas_call(
        kernel,
        out_shape=outs,
        in_specs=[where(k, far) for k in range(len(args))],
        out_specs=tuple(where(k, far_outs) for k in range(len(outs))),
        scratch_shapes=list(scratch),
        compiler_params=pltpu.CompilerParams(vmem_limit_bytes=VMEM_LIMIT),
        name=name,
    )(*args)


def out(shape, dtype):
    return jax.ShapeDtypeStruct(shape, dtype)


def lanes(shape):
    return lax.broadcasted_iota(jnp.int32, shape, len(shape) - 1)


def rows(shape):
    return lax.broadcasted_iota(jnp.int32, shape, len(shape) - 2)


def roll(x, by, axis=1):
    by = by % x.shape[axis]
    return x if by == 0 else pltpu.roll(x, by, axis)


def place(chunks, refs):
    me = lax.axis_index("tm")
    for hop, ref in enumerate(refs):
        ref[...] = chunks[me ^ hop]


def gather(chunks, refs):
    me = lax.axis_index("tm")
    for hop, ref in enumerate(refs):
        chunks[me ^ hop] = ref[...]


def pack_kernel(cot_ref, *refs):
    chunks = refs[-1]
    n = chunks.shape[0]
    low = lanes((1, 128)) < TOUT
    for f2 in range(F // 2):
        for tile in range(n // 2):
            a = cot_ref[2 * f2, :, 128 * tile : 128 * (tile + 1)]
            b = cot_ref[2 * f2 + 1, :, 128 * tile : 128 * (tile + 1)]
            chunks[2 * tile, f2] = jnp.where(low, a, roll(b, TOUT))
            chunks[2 * tile + 1, f2] = jnp.where(low, roll(a, TOUT), b)
    place(chunks, refs[:-1])


def tail_kernel(strain_ref, halo_out, scratch):
    group = lanes((1, 128)) // HALO
    for i4 in range(F // 4):
        tile = roll(strain_ref[4 * i4], HALO)
        for e in range(1, 4):
            tile = jnp.where(group == e, roll(strain_ref[4 * i4 + e], HALO * (e + 1)), tile)
        turned = tile.T.astype(F32)
        for e in range(4):
            scratch[pl.ds(4 * i4 + e, HALO, stride=F), :] = turned[HALO * e : HALO * (e + 1)]
    halo_out[...] = scratch[...].astype(BF)


def turn_kernel(strain_ref, out_ref, scratch):
    for i in range(F):
        scratch[pl.ds(i, STEPS, stride=F), :] = strain_ref[i].T.astype(F32)
    out_ref[...] = scratch[...].astype(BF)


def weight_kernel(time_ref, fiber_ref, w_out, v_out, d_out, dt_out, scratch):
    for o4 in range(F // 4):
        turned = time_ref[4 * o4 : 4 * (o4 + 1)].astype(F32).reshape(4 * F, TAPS)
        turned = jnp.concatenate([turned, jnp.zeros((4 * F, 128 - TAPS), F32)], axis=1).T[0:TAPS]
        for e in range(4):
            scratch[pl.ds(4 * o4 + e, TAPS, stride=F), :] = roll(turned, -F * e)
    group = lanes((1, 128)) // F
    tiles = []
    for k4 in range(TAPS // 4):
        tile = scratch[F * 4 * k4 : F * (4 * k4 + 1)]
        for e in range(1, 4):
            tile = jnp.where(group == e, roll(scratch[F * (4 * k4 + e) : F * (4 * k4 + e + 1)], F * e), tile)
        tiles.append(tile)
    tiles.append(jnp.zeros((F, WIN - TAPS * F), F32))
    base = jnp.concatenate(tiles, axis=1)
    for t in range(TB):
        w_out[F * t : F * (t + 1)] = roll(base, 2 * F * (t + 1)).astype(BF)
    size, step = TB * F, 2 * TB * F
    for a in range(3):
        v_out[:, size * a : size * (a + 1)] = w_out[:, step * (2 - a) : step * (3 - a)].T
    taps = fiber_ref[...]
    spread = (lax.broadcasted_iota(jnp.int32, (F, GROWS), 1) % F == lax.broadcasted_iota(jnp.int32, (F, GROWS), 0)).astype(BF)
    wide = jnp.dot(taps, spread, preferred_element_type=F32).astype(BF)
    row = lax.broadcasted_iota(jnp.int32, (GROWS, GROWS), 0)
    col = lax.broadcasted_iota(jnp.int32, (GROWS, GROWS), 1)
    together = (row // PER) == (col // PER)
    which = lax.broadcasted_iota(jnp.int32, (GROWS, KF * PER), 1)
    feat = lax.broadcasted_iota(jnp.int32, (GROWS, KF * PER), 0) % PER
    for m in range(KF):
        pick = (which == PER * m + feat).astype(BF)
        block = jnp.where(together, jnp.dot(pick, wide, preferred_element_type=F32), 0.0)
        dt_out[:, GROWS * m : GROWS * (m + 1)] = block.astype(BF)
        d_out[:, GROWS * m : GROWS * (m + 1)] = block.T.astype(BF)


def pack_edges(read):
    group = lanes((1, 128)) // 8
    packed = roll(read(0), REACH)
    for g in range(1, NG):
        packed = jnp.where(group == g, roll(read(g), 8 * g + REACH), packed)
    return packed


def edges_of(before_ref, after_ref):
    me, size = lax.axis_index("fiber"), lax.axis_size("fiber")
    first = lanes((1, 128)) % 8 < REACH
    keep_before = jnp.where(me > 0, 1.0, 0.0).astype(F32)
    keep_after = jnp.where(me < size - 1, 1.0, 0.0).astype(F32)
    both = jnp.where(first, before_ref[...].astype(F32) * keep_before, after_ref[...].astype(F32) * keep_after)
    return both.astype(BF)


def shifted_stack(tile, edges, g, shifts):
    around = roll(edges, -(8 * g + REACH))
    lane = lanes((1, 128))
    pieces = []
    for by in shifts:
        if by > 0:
            pieces.append(roll(jnp.where(lane < by, around, tile), -by))
        elif by < 0:
            pieces.append(roll(jnp.where(lane >= CH + by, around, tile), -by))
        else:
            pieces.append(tile)
    return jnp.concatenate(pieces, axis=0)


def window(early_ref, main_ref, b, size):
    start = 2 * TB * F * b
    early = early_ref.shape[0]
    if start >= early:
        return main_ref[start - early : start - early + size]
    return jnp.concatenate([early_ref[start:early], main_ref[0 : size - (early - start)]], axis=0)


def inner_kernel(halo_ref, strain_ref, w_ref, u_out, edge_out):
    size = TB * F
    for b in range(0, TOUT // TB, 2):
        pair = jnp.concatenate([window(halo_ref, strain_ref, b + k, WIN) for k in range(2)], axis=1)
        u = jnp.dot(w_ref[...], pair, preferred_element_type=F32)
        for k in range(2):
            u_out[size * (b + k) : size * (b + k + 1)] = u[:, CH * k : CH * (k + 1)].astype(BF)
    edge_out[...] = pack_edges(lambda g: u_out[GROWS * g : GROWS * (g + 1)])


def forward_kernel(u_ref, before_ref, after_ref, d_ref, slope_out, *refs):
    chunks, scratch = refs[-2:]
    edges = edges_of(before_ref, after_ref)
    for g in range(0, NG, 2):
        pair = jnp.concatenate(
            [
                shifted_stack(
                    u_ref[GROWS * (g + k) : GROWS * (g + k + 1)], edges, g + k, range(-REACH, REACH + 1)
                )
                for k in range(2)
            ],
            axis=1,
        )
        z = jnp.dot(d_ref[...], pair, preferred_element_type=F32).astype(BF).astype(F32)
        half = 0.5 * (1.0 + lax.erf(z * (1.0 / math.sqrt(2.0))))
        slope = half + z * jnp.exp(-0.5 * z * z) * (1.0 / math.sqrt(2.0 * math.pi))
        act = z * half
        for k in range(2):
            where = slice(GROWS * (g + k), GROWS * (g + k + 1))
            scratch[where] = act[:, CH * k : CH * (k + 1)]
            slope_out[where] = slope[:, CH * k : CH * (k + 1)]
    n, _, local, _ = chunks.shape
    for f2 in range(F // 2):
        both = jnp.concatenate([scratch[pl.ds(2 * f2 + e, TOUT, stride=F), :] for e in range(2)], axis=0)
        turned = both.astype(BF).T
        for q in range(n):
            chunks[q, f2] = turned[local * q : local * (q + 1)]
    place(chunks, refs[:-2])


def slope_kernel(slope_ref, *refs):
    dz_out, edge_out, chunks, scratch = refs[-4:]
    gather(chunks, refs[:-4])
    local = chunks.shape[2]
    for f2 in range(F // 2):
        if local % 16 == 0:
            turned = chunks[:, f2].reshape(CH, 128).T.astype(F32)
        else:
            turned = chunks[:, f2].astype(F32).reshape(CH, 128).T
        for e in range(2):
            scratch[pl.ds(2 * f2 + e, TOUT, stride=F), :] = turned[TOUT * e : TOUT * (e + 1)]
    dz_out[...] = (scratch[...] * slope_ref[...]).astype(BF)
    edge_out[...] = pack_edges(lambda g: dz_out[GROWS * g : GROWS * (g + 1)])


def backward_kernel(dz_ref, before_ref, after_ref, dt_ref, u_ref, halo_ref, strain_ref, du_out, grad_out):
    edges = edges_of(before_ref, after_ref)
    taps = jnp.zeros((GROWS, KF * GROWS), F32)
    for g in range(0, NG, 2):
        stacks = [
            shifted_stack(
                dz_ref[GROWS * (g + k) : GROWS * (g + k + 1)],
                edges,
                g + k,
                [REACH - m for m in range(KF)],
            )
            for k in range(2)
        ]
        pair = jnp.concatenate(stacks, axis=1)
        du = jnp.dot(dt_ref[...], pair, preferred_element_type=F32).astype(BF)
        u = jnp.concatenate([u_ref[GROWS * (g + k) : GROWS * (g + k + 1)] for k in range(2)], axis=1)
        taps = taps + lax.dot_general(u, pair, NT, preferred_element_type=F32)
        for k in range(2):
            du_out[GROWS * (g + k) : GROWS * (g + k + 1)] = du[:, CH * k : CH * (k + 1)]
    lane = lanes((1, KF * GROWS))
    step = (lane % GROWS) // F
    kept = jnp.where(step == 0, taps[0:F], 0.0)
    for t in range(1, TG):
        kept = jnp.where(step == t, taps[F * t : F * (t + 1)], kept)
    feat = lane % F
    row = rows((F, 1))
    lines = []
    for j in range(PER):
        lines.append(jnp.sum(jnp.where(row == feat // PER * PER + j, kept, 0.0), axis=0, keepdims=True))
    lines = jnp.concatenate(lines + [jnp.zeros((8 - PER, KF * GROWS), F32)], axis=0)
    tiles = []
    for top in range(0, KF, TG):
        tile = jnp.zeros((8, GROWS), F32)
        for m in range(top, min(KF, top + TG)):
            line = lines[:, GROWS * m : GROWS * (m + 1)]
            total = line
            for t in range(1, TG):
                total = total + roll(line, F * t)
            tile = jnp.where(lanes((1, GROWS)) // F == m - top, total, tile)
        tiles.append(tile)
    size = TB * F
    wide = jnp.zeros((size, WIN), F32)
    for b in range(0, TOUT // TB, 2):
        left = jnp.concatenate([du_out[size * (b + k) : size * (b + k + 1)] for k in range(2)], axis=1)
        right = jnp.concatenate([window(halo_ref, strain_ref, b + k, WIN) for k in range(2)], axis=1)
        wide = wide + lax.dot_general(left, right, NT, preferred_element_type=F32)
    total = jnp.zeros((F, WIN), F32)
    for t in range(TB):
        total = total + roll(wide[F * t : F * (t + 1)], -2 * F * (t + 1))
    grad_out[0:F] = total[:, 0 : TAPS * F]
    tiles.append(jnp.zeros((8, TAPS * F - len(tiles) * GROWS), F32))
    grad_out[F : F + 8] = jnp.concatenate(tiles, axis=1)


def signal_kernel(du_ref, late_ref, v_ref, grad_out, scratch, ready, sems):
    size = TB * F
    last = TOUT * F

    def rows_of(b):
        start, stop = size * b, size * b + VWIN
        if stop <= last:
            return du_ref[start:stop]
        return jnp.concatenate([du_ref[start:last], late_ref[0 : stop - last]], axis=0)

    step = 2 * TB * F
    for b in range(0, TOUT // TB, 2):
        pair = jnp.concatenate([rows_of(b + k) for k in range(2)], axis=1)
        part = jnp.dot(v_ref[...], pair, preferred_element_type=F32)
        for k in range(2):
            scratch[step * (b + k) : step * (b + k + 1)] = part[:, CH * k : CH * (k + 1)]
    each = F // 4
    copies = []
    for k in range(4):
        for i in range(each * k, each * (k + 1)):
            ready[i] = scratch[pl.ds(i, STEPS, stride=F), :].astype(BF).T
        part = pl.ds(each * k, each)
        copies.append(pltpu.make_async_copy(ready.at[part], grad_out.at[part], sems.at[k]))
        copies[-1].start()
    for copy in copies:
        copy.wait()


def unpack_kernel(*refs):
    act_out, chunks = refs[-2:]
    gather(chunks, refs[:-2])
    n = chunks.shape[0]
    low = lanes((1, 128)) < TOUT
    for f2 in range(F // 2):
        for tile in range(n // 2):
            a = chunks[2 * tile, f2]
            b = chunks[2 * tile + 1, f2]
            where = slice(128 * tile, 128 * (tile + 1))
            act_out[2 * f2, :, where] = jnp.where(low, a, roll(b, TOUT))
            act_out[2 * f2 + 1, :, where] = jnp.where(low, roll(a, TOUT), b)


def finish_kernel(scale, mine_ref, other_ref, time_out, fiber_out, scratch):
    total = (mine_ref[...].astype(F32) + other_ref[...].astype(F32)) * scale
    for k in range(TAPS):
        tile = total[0:F, 128 * (k // 4) : 128 * (k // 4 + 1)]
        scratch[pl.ds(k, F, stride=TAPS), :] = roll(tile, -F * (k % 4))
    for o4 in range(F // 4):
        turned = scratch[4 * TAPS * o4 : 4 * TAPS * (o4 + 1)].T[0:F]
        for e in range(4):
            time_out[4 * o4 + e] = roll(turned, -TAPS * e)[:, 0:TAPS]
    for m in range(KF):
        tile = total[F : F + 8, 128 * (m // 4) : 128 * (m // 4 + 1)]
        fiber_out[m] = roll(tile, -F * (m % 4))[0:PER, 0:F]


def exchanged(chunks):
    size = len(chunks)
    got = [chunks[0]]
    for hop in range(1, size):
        got.append(lax.ppermute(chunks[hop], "tm", [(i, i ^ hop) for i in range(size)]))
    return got


def neighbours(array, axis):
    size = lax.axis_size(axis)
    if size == 2:
        other = lax.ppermute(array, axis, [(0, 1), (1, 0)])
        return other, other
    before = lax.ppermute(array, axis, [(i, i + 1) for i in range(size - 1)])
    after = lax.ppermute(array, axis, [(i + 1, i) for i in range(size - 1)])
    return before, after


def paired(array, axis, hop):
    mine = array.astype(BF)
    return mine, lax.ppermute(mine, axis, [(i, i ^ hop) for i in range(lax.axis_size(axis))])


def on_device(strain, time_kernel, fiber_kernel, cotangent):
    n = lax.axis_size("tm")
    size = lax.axis_size("rep") * CH * lax.axis_size("fiber") * TOUT * n
    scale = 1.0 / math.sqrt(size)
    local = cotangent.shape[3]
    x = strain[0]
    chunk = (F // 2, local, 128)
    packed = (n,) + chunk
    flat = (TOUT * F, CH)
    (tail,) = call(
        tail_kernel, (out((HALO * F, CH), BF),), x, scratch=[pltpu.VMEM((HALO * F, CH), F32)], name="tail"
    )
    halo = lax.ppermute(tail, "tm", [(i, i + 1) for i in range(n - 1)])
    cot, tail = lax.optimization_barrier((cotangent[0, :, 0], tail))
    sent = call(pack_kernel, (out(chunk, BF),) * n, cot, scratch=[pltpu.VMEM(packed, BF)], name="pack")
    upstream = exchanged(sent)

    w, v, d, dt = call(
        weight_kernel,
        (
            out((TB * F, WIN), BF),
            out((2 * TB * F, VWIN), BF),
            out((GROWS, KF * GROWS), BF),
            out((GROWS, KF * GROWS), BF),
        ),
        time_kernel,
        jnp.transpose(fiber_kernel, (2, 1, 0)).reshape(KF * PER, F),
        scratch=[pltpu.VMEM((TAPS * F, 128), F32)],
        name="weights",
    )
    (turned,) = call(
        turn_kernel, (out((STEPS * F, CH), BF),), x, scratch=[pltpu.VMEM((STEPS * F, CH), F32)], name="turn"
    )
    u, u_edge = call(
        inner_kernel,
        (out(flat, BF), out((GROWS, CH), BF)),
        halo,
        turned,
        w,
        name="inner",
    )
    before, after = neighbours(u_edge, "fiber")
    slope, *act = call(
        forward_kernel,
        (out(flat, F32),) + (out(chunk, BF),) * n,
        u,
        before,
        after,
        d,
        scratch=[pltpu.VMEM(packed, BF), pltpu.VMEM(flat, F32)],
        name="forward",
    )
    act = exchanged(act)
    dz, dz_edge = call(
        slope_kernel,
        (out(flat, BF), out((GROWS, CH), BF)),
        slope,
        *upstream,
        scratch=[pltpu.VMEM(packed, BF), pltpu.VMEM(flat, F32)],
        name="slope",
    )
    before, after = neighbours(dz_edge, "fiber")
    du, grads = call(
        backward_kernel,
        (out(flat, BF), out((F + 8, TAPS * F), F32)),
        dz,
        before,
        after,
        dt,
        u,
        halo,
        turned,
        name="backward",
    )
    hops = [(axis, 1 << k) for axis in ("rep", "fiber", "tm") for k in range((lax.axis_size(axis) - 1).bit_length())]
    head = du[0 : LATE * F]
    for step, (axis, hop) in enumerate(hops):
        if step == 0:
            grads, *act = lax.optimization_barrier((grads, *act))
            (activation,) = call(
                unpack_kernel, (out((F, local, n * TOUT), BF),), *act, scratch=[pltpu.VMEM(packed, BF)], name="unpack"
            )
        if step == 2:
            grads, head, activation = lax.optimization_barrier((grads, head, activation))
        mine, other = paired(grads, axis, hop)
        if step < len(hops) - 1:
            grads = mine.astype(F32) + other.astype(F32)
    late = lax.ppermute(head, "tm", [(i + 1, i) for i in range(n - 1)])
    (strain_grad,) = call(
        signal_kernel,
        (out((F, CH, STEPS), BF),),
        du,
        late,
        v,
        scratch=[
            pltpu.VMEM((STEPS * F, CH), F32),
            pltpu.VMEM((F, CH, STEPS), BF),
            pltpu.SemaphoreType.DMA((4,)),
        ],
        name="signal",
        far_outs=(0,),
    )
    time_grad, fiber_grad = call(
        functools.partial(finish_kernel, scale),
        (out((F, F, TAPS), F32), out((KF, PER, F), F32)),
        mine,
        other,
        scratch=[pltpu.VMEM((F * TAPS, 128), F32)],
        name="finish",
    )
    return activation[None, :, None], strain_grad[None], time_grad, jnp.transpose(fiber_grad, (2, 1, 0))


def solution(mesh):
    placed = (
        P(("parts", "rep"), None, "fiber", "tm"),
        P(),
        P(),
        P(("parts", "rep"), None, "fiber", "tm", None),
    )
    return jax.shard_map(
        on_device,
        mesh=mesh,
        in_specs=placed,
        out_specs=(
            P(("parts", "rep"), None, "fiber", "tm", None),
            P(("parts", "rep"), None, "fiber", "tm"),
            P("parts", None, None),
            P("parts", None, None),
        ),
        check_vma=False,
    )
```

```python
import functools
import math

import jax
import jax.numpy as jnp
from jax import lax
from jax.experimental import pallas as pl
from jax.experimental.pallas import tpu as pltpu
from jax.sharding import PartitionSpec as P

F = 32
PER = 4
TAPS = 32
KF = 9
REACH = KF // 2
CH = 128
STEPS = 128
TOUT = STEPS // 2
HALO = 32
TB = 8
WIN = (2 * TB + TAPS) * F
TG = 4
GROWS = TG * F
NG = TOUT // TG
VWIN = 24 * F
CORES = [(0, 1), (1, 0)]
HALF = TAPS * F // 2
EARLY = STEPS - HALO
LATE = 16
BF = jnp.bfloat16
F32 = jnp.float32
NT = (((1,), (1,)), ((), ()))
VMEM_LIMIT = 16 * 1024 * 1024


def call(kernel, outs, *args, scratch=(), name=None, far=(), far_outs=()):
    where = lambda k, away: pl.BlockSpec(memory_space=pltpu.HBM if k in away else pltpu.VMEM)
    return pl.pallas_call(
        kernel,
        out_shape=outs,
        in_specs=[where(k, far) for k in range(len(args))],
        out_specs=tuple(where(k, far_outs) for k in range(len(outs))),
        scratch_shapes=list(scratch),
        compiler_params=pltpu.CompilerParams(vmem_limit_bytes=VMEM_LIMIT),
        name=name,
    )(*args)


def out(shape, dtype):
    return jax.ShapeDtypeStruct(shape, dtype)


def lanes(shape):
    return lax.broadcasted_iota(jnp.int32, shape, len(shape) - 1)


def rows(shape):
    return lax.broadcasted_iota(jnp.int32, shape, len(shape) - 2)


def roll(x, by, axis=1):
    by = by % x.shape[axis]
    return x if by == 0 else pltpu.roll(x, by, axis)


def place(chunks, refs):
    me = lax.axis_index("tm")
    for hop, ref in enumerate(refs):
        ref[...] = chunks[me ^ hop]


def gather(chunks, refs):
    me = lax.axis_index("tm")
    for hop, ref in enumerate(refs):
        chunks[me ^ hop] = ref[...]


def pack_kernel(cot_ref, *refs):
    chunks = refs[-1]
    n = chunks.shape[0]
    low = lanes((1, 128)) < TOUT
    for f2 in range(F // 2):
        for tile in range(n // 2):
            a = cot_ref[2 * f2, :, 128 * tile : 128 * (tile + 1)]
            b = cot_ref[2 * f2 + 1, :, 128 * tile : 128 * (tile + 1)]
            chunks[2 * tile, f2] = jnp.where(low, a, roll(b, TOUT))
            chunks[2 * tile + 1, f2] = jnp.where(low, roll(a, TOUT), b)
    place(chunks, refs[:-1])


def tail_kernel(strain_ref, halo_out, strain_out, scratch, sems):
    each = F // 4
    copies = [
        pltpu.make_async_copy(strain_ref.at[pl.ds(each * k, each)], strain_out.at[pl.ds(each * k, each)], sems.at[k])
        for k in range(4)
    ]
    for copy in copies:
        copy.start()
    group = lanes((1, 128)) // HALO
    for i4 in range(F // 4):
        if i4 % 2 == 0:
            copies[i4 // 2].wait()
        tile = roll(strain_out[4 * i4], HALO)
        for e in range(1, 4):
            tile = jnp.where(group == e, roll(strain_out[4 * i4 + e], HALO * (e + 1)), tile)
        turned = tile.T.astype(F32)
        for e in range(4):
            scratch[pl.ds(4 * i4 + e, HALO, stride=F), :] = turned[HALO * e : HALO * (e + 1)]
    halo_out[...] = scratch[...].astype(BF)


def turn_kernel(strain_ref, out_ref, scratch):
    for i in range(F):
        scratch[pl.ds(i, STEPS, stride=F), :] = strain_ref[i].T.astype(F32)
    out_ref[...] = scratch[...].astype(BF)


def weight_kernel(time_ref, fiber_ref, w_out, v_out, d_out, dt_out, scratch):
    for o4 in range(F // 4):
        turned = time_ref[4 * o4 : 4 * (o4 + 1)].astype(F32).reshape(4 * F, TAPS)
        turned = jnp.concatenate([turned, jnp.zeros((4 * F, 128 - TAPS), F32)], axis=1).T[0:TAPS]
        for e in range(4):
            scratch[pl.ds(4 * o4 + e, TAPS, stride=F), :] = roll(turned, -F * e)
    group = lanes((1, 128)) // F
    tiles = []
    for k4 in range(TAPS // 4):
        tile = scratch[F * 4 * k4 : F * (4 * k4 + 1)]
        for e in range(1, 4):
            tile = jnp.where(group == e, roll(scratch[F * (4 * k4 + e) : F * (4 * k4 + e + 1)], F * e), tile)
        tiles.append(tile)
    tiles.append(jnp.zeros((F, WIN - TAPS * F), F32))
    base = jnp.concatenate(tiles, axis=1)
    for t in range(TB):
        w_out[F * t : F * (t + 1)] = roll(base, 2 * F * (t + 1)).astype(BF)
    size, step = TB * F, 2 * TB * F
    for a in range(3):
        v_out[:, size * a : size * (a + 1)] = w_out[:, step * (2 - a) : step * (3 - a)].T
    taps = fiber_ref[...]
    spread = (lax.broadcasted_iota(jnp.int32, (F, GROWS), 1) % F == lax.broadcasted_iota(jnp.int32, (F, GROWS), 0)).astype(BF)
    wide = jnp.dot(taps, spread, preferred_element_type=F32).astype(BF)
    row = lax.broadcasted_iota(jnp.int32, (GROWS, GROWS), 0)
    col = lax.broadcasted_iota(jnp.int32, (GROWS, GROWS), 1)
    together = (row // PER) == (col // PER)
    which = lax.broadcasted_iota(jnp.int32, (GROWS, KF * PER), 1)
    feat = lax.broadcasted_iota(jnp.int32, (GROWS, KF * PER), 0) % PER
    for m in range(KF):
        pick = (which == PER * m + feat).astype(BF)
        block = jnp.where(together, jnp.dot(pick, wide, preferred_element_type=F32), 0.0)
        dt_out[:, GROWS * m : GROWS * (m + 1)] = block.astype(BF)
        d_out[:, GROWS * m : GROWS * (m + 1)] = block.T.astype(BF)


def pack_edges(read):
    group = lanes((1, 128)) // 8
    packed = roll(read(0), REACH)
    for g in range(1, NG):
        packed = jnp.where(group == g, roll(read(g), 8 * g + REACH), packed)
    return packed


def edges_of(before_ref, after_ref):
    me, size = lax.axis_index("fiber"), lax.axis_size("fiber")
    first = lanes((1, 128)) % 8 < REACH
    keep_before = jnp.where(me > 0, 1.0, 0.0).astype(F32)
    keep_after = jnp.where(me < size - 1, 1.0, 0.0).astype(F32)
    both = jnp.where(first, before_ref[...].astype(F32) * keep_before, after_ref[...].astype(F32) * keep_after)
    return both.astype(BF)


def shifted_stack(tile, edges, g, shifts):
    around = roll(edges, -(8 * g + REACH))
    lane = lanes((1, 128))
    pieces = []
    for by in shifts:
        if by > 0:
            pieces.append(roll(jnp.where(lane < by, around, tile), -by))
        elif by < 0:
            pieces.append(roll(jnp.where(lane >= CH + by, around, tile), -by))
        else:
            pieces.append(tile)
    return jnp.concatenate(pieces, axis=0)


def window(early_ref, main_ref, b, size):
    start = 2 * TB * F * b
    early = early_ref.shape[0]
    if start >= early:
        return main_ref[start - early : start - early + size]
    return jnp.concatenate([early_ref[start:early], main_ref[0 : size - (early - start)]], axis=0)


def inner_kernel(halo_ref, strain_ref, w_ref, u_out, edge_out):
    size = TB * F
    for b in range(0, TOUT // TB, 2):
        pair = jnp.concatenate([window(halo_ref, strain_ref, b + k, WIN) for k in range(2)], axis=1)
        u = jnp.dot(w_ref[...], pair, preferred_element_type=F32)
        for k in range(2):
            u_out[size * (b + k) : size * (b + k + 1)] = u[:, CH * k : CH * (k + 1)].astype(BF)
    edge_out[...] = pack_edges(lambda g: u_out[GROWS * g : GROWS * (g + 1)])


def forward_kernel(u_ref, before_ref, after_ref, d_ref, slope_out, *refs):
    chunks, scratch = refs[-2:]
    edges = edges_of(before_ref, after_ref)
    for g in range(0, NG, 2):
        pair = jnp.concatenate(
            [
                shifted_stack(
                    u_ref[GROWS * (g + k) : GROWS * (g + k + 1)], edges, g + k, range(-REACH, REACH + 1)
                )
                for k in range(2)
            ],
            axis=1,
        )
        z = jnp.dot(d_ref[...], pair, preferred_element_type=F32).astype(BF).astype(F32)
        half = 0.5 * (1.0 + lax.erf(z * (1.0 / math.sqrt(2.0))))
        slope = half + z * jnp.exp(-0.5 * z * z) * (1.0 / math.sqrt(2.0 * math.pi))
        act = z * half
        for k in range(2):
            where = slice(GROWS * (g + k), GROWS * (g + k + 1))
            scratch[where] = act[:, CH * k : CH * (k + 1)]
            slope_out[where] = slope[:, CH * k : CH * (k + 1)]
    n, _, local, _ = chunks.shape
    for f2 in range(F // 2):
        both = jnp.concatenate([scratch[pl.ds(2 * f2 + e, TOUT, stride=F), :] for e in range(2)], axis=0)
        turned = both.astype(BF).T
        for q in range(n):
            chunks[q, f2] = turned[local * q : local * (q + 1)]
    place(chunks, refs[:-2])


def slope_kernel(slope_ref, *refs):
    dz_out, edge_out, chunks, scratch = refs[-4:]
    gather(chunks, refs[:-4])
    local = chunks.shape[2]
    for f2 in range(F // 2):
        if local % 16 == 0:
            turned = chunks[:, f2].reshape(CH, 128).T.astype(F32)
        else:
            turned = chunks[:, f2].astype(F32).reshape(CH, 128).T
        for e in range(2):
            scratch[pl.ds(2 * f2 + e, TOUT, stride=F), :] = turned[TOUT * e : TOUT * (e + 1)]
    dz_out[...] = (scratch[...] * slope_ref[...]).astype(BF)
    edge_out[...] = pack_edges(lambda g: dz_out[GROWS * g : GROWS * (g + 1)])


def backward_kernel(dz_ref, before_ref, after_ref, dt_ref, u_ref, halo_ref, strain_ref, du_out, keep_out, give_out):
    edges = edges_of(before_ref, after_ref)
    taps = jnp.zeros((GROWS, KF * GROWS), F32)
    for g in range(0, NG, 2):
        stacks = [
            shifted_stack(
                dz_ref[GROWS * (g + k) : GROWS * (g + k + 1)],
                edges,
                g + k,
                [REACH - m for m in range(KF)],
            )
            for k in range(2)
        ]
        pair = jnp.concatenate(stacks, axis=1)
        du = jnp.dot(dt_ref[...], pair, preferred_element_type=F32).astype(BF)
        u = jnp.concatenate([u_ref[GROWS * (g + k) : GROWS * (g + k + 1)] for k in range(2)], axis=1)
        taps = taps + lax.dot_general(u, pair, NT, preferred_element_type=F32)
        for k in range(2):
            du_out[GROWS * (g + k) : GROWS * (g + k + 1)] = du[:, CH * k : CH * (k + 1)]
    lane = lanes((1, KF * GROWS))
    step = (lane % GROWS) // F
    kept = jnp.where(step == 0, taps[0:F], 0.0)
    for t in range(1, TG):
        kept = jnp.where(step == t, taps[F * t : F * (t + 1)], kept)
    feat = lane % F
    row = rows((F, 1))
    lines = []
    for j in range(PER):
        lines.append(jnp.sum(jnp.where(row == feat // PER * PER + j, kept, 0.0), axis=0, keepdims=True))
    lines = jnp.concatenate(lines + [jnp.zeros((8 - PER, KF * GROWS), F32)], axis=0)
    tiles = []
    for top in range(0, KF, TG):
        tile = jnp.zeros((8, GROWS), F32)
        for m in range(top, min(KF, top + TG)):
            line = lines[:, GROWS * m : GROWS * (m + 1)]
            total = line
            for t in range(1, TG):
                total = total + roll(line, F * t)
            tile = jnp.where(lanes((1, GROWS)) // F == m - top, total, tile)
        tiles.append(tile)
    size = TB * F
    wide = jnp.zeros((size, WIN), F32)
    for b in range(0, TOUT // TB, 2):
        left = jnp.concatenate([du_out[size * (b + k) : size * (b + k + 1)] for k in range(2)], axis=1)
        right = jnp.concatenate([window(halo_ref, strain_ref, b + k, WIN) for k in range(2)], axis=1)
        wide = wide + lax.dot_general(left, right, NT, preferred_element_type=F32)
    total = jnp.zeros((F, WIN), F32)
    for t in range(TB):
        total = total + roll(wide[F * t : F * (t + 1)], -2 * F * (t + 1))
    tiles.append(jnp.zeros((8, TAPS * F - len(tiles) * GROWS), F32))
    total = jnp.concatenate([total[:, 0 : TAPS * F], jnp.concatenate(tiles, axis=1)], axis=0)
    lower, upper = total[:, 0:HALF], total[:, HALF : 2 * HALF]
    first = lax.axis_index("rep") == 0
    keep_out[...] = jnp.where(first, lower, upper)
    give_out[...] = jnp.where(first, upper, lower).astype(BF)


def signal_blocks(v_ref, rows_of, blocks, scratch):
    step = 2 * TB * F
    for b in range(0, len(blocks), 2):
        pair = jnp.concatenate([rows_of(blocks[b + k]) for k in range(2)], axis=1)
        part = jnp.dot(v_ref[...], pair, preferred_element_type=F32)
        for k in range(2):
            scratch[step * (b + k) : step * (b + k + 1)] = part[:, CH * k : CH * (k + 1)]


def early_kernel(du_ref, v_ref, early_out, scratch):
    size = TB * F
    scratch[EARLY * F :] = jnp.zeros(((STEPS - EARLY) * F, CH), F32)
    signal_blocks(v_ref, lambda b: du_ref[size * b : size * b + VWIN], range(TOUT // TB - 2), scratch)
    for i in range(F):
        early_out[i] = scratch[pl.ds(i, STEPS, stride=F), :].astype(BF).T


def signal_kernel(du_ref, late_ref, v_ref, early_ref, grad_out, scratch, ready, sems):
    size = TB * F
    last = TOUT * F

    def rows_of(b):
        start, stop = size * b, size * b + VWIN
        return jnp.concatenate([du_ref[start:last], late_ref[0 : stop - last]], axis=0)

    signal_blocks(v_ref, rows_of, range(TOUT // TB - 2, TOUT // TB), scratch)
    count = STEPS - EARLY
    ends = lanes((1, 128)) >= EARLY
    copies = []
    for i4 in range(F // 4):
        four = jnp.concatenate([scratch[pl.ds(4 * i4 + e, count, stride=F), :] for e in range(4)], axis=0)
        turned = four.astype(BF).T
        for e in range(4):
            ready[4 * i4 + e] = jnp.where(ends, roll(turned, EARLY - count * e), early_ref[4 * i4 + e])
        if i4 % 2 == 1:
            part = pl.ds(4 * (i4 - 1), 8)
            copies.append(pltpu.make_async_copy(ready.at[part], grad_out.at[part], sems.at[i4 // 2]))
            copies[-1].start()
    for copy in copies:
        copy.wait()


def unpack_kernel(*refs):
    act_out, chunks = refs[-2:]
    gather(chunks, refs[:-2])
    n = chunks.shape[0]
    low = lanes((1, 128)) < TOUT
    for f2 in range(F // 2):
        for tile in range(n // 2):
            a = chunks[2 * tile, f2]
            b = chunks[2 * tile + 1, f2]
            where = slice(128 * tile, 128 * (tile + 1))
            act_out[2 * f2, :, where] = jnp.where(low, a, roll(b, TOUT))
            act_out[2 * f2 + 1, :, where] = jnp.where(low, roll(a, TOUT), b)


def finish_kernel(scale, mine_ref, other_ref, time_out, fiber_out, scratch):
    first = lax.axis_index("rep") == 0
    mine, other = mine_ref[...], other_ref[...]
    total = jnp.concatenate([jnp.where(first, mine, other), jnp.where(first, other, mine)], axis=1) * scale
    for k in range(TAPS):
        tile = total[0:F, 128 * (k // 4) : 128 * (k // 4 + 1)]
        scratch[pl.ds(k, F, stride=TAPS), :] = roll(tile, -F * (k % 4))
    for o4 in range(F // 4):
        turned = scratch[4 * TAPS * o4 : 4 * TAPS * (o4 + 1)].T[0:F]
        for e in range(4):
            time_out[4 * o4 + e] = roll(turned, -TAPS * e)[:, 0:TAPS]
    for m in range(KF):
        tile = total[F : F + 8, 128 * (m // 4) : 128 * (m // 4 + 1)]
        fiber_out[m] = roll(tile, -F * (m % 4))[0:PER, 0:F]


def exchanged(chunks):
    size = len(chunks)
    got = [chunks[0]]
    for hop in range(1, size):
        got.append(lax.ppermute(chunks[hop], "tm", [(i, i ^ hop) for i in range(size)]))
    return got


def neighbours(array, axis):
    size = lax.axis_size(axis)
    if size == 2:
        other = lax.ppermute(array, axis, [(0, 1), (1, 0)])
        return other, other
    before = lax.ppermute(array, axis, [(i, i + 1) for i in range(size - 1)])
    after = lax.ppermute(array, axis, [(i + 1, i) for i in range(size - 1)])
    return before, after


def paired(array, axis, hop):
    mine = array.astype(BF)
    return mine, lax.ppermute(mine, axis, [(i, i ^ hop) for i in range(lax.axis_size(axis))])


def on_device(strain, time_kernel, fiber_kernel, cotangent):
    n = lax.axis_size("tm")
    size = lax.axis_size("rep") * CH * lax.axis_size("fiber") * TOUT * n
    scale = 1.0 / math.sqrt(size)
    local = cotangent.shape[3]
    x = strain[0]
    chunk = (F // 2, local, 128)
    packed = (n,) + chunk
    flat = (TOUT * F, CH)
    tail, x = call(
        tail_kernel,
        (out((HALO * F, CH), BF), out(x.shape, BF)),
        x,
        scratch=[pltpu.VMEM((HALO * F, CH), F32), pltpu.SemaphoreType.DMA((4,))],
        name="tail",
        far=(0,),
    )
    halo = lax.ppermute(tail, "tm", [(i, i + 1) for i in range(n - 1)])
    cot, tail = lax.optimization_barrier((cotangent[0, :, 0], tail))
    sent = call(pack_kernel, (out(chunk, BF),) * n, cot, scratch=[pltpu.VMEM(packed, BF)], name="pack")

    w, v, d, dt = call(
        weight_kernel,
        (
            out((TB * F, WIN), BF),
            out((2 * TB * F, VWIN), BF),
            out((GROWS, KF * GROWS), BF),
            out((GROWS, KF * GROWS), BF),
        ),
        time_kernel,
        jnp.transpose(fiber_kernel, (2, 1, 0)).reshape(KF * PER, F),
        scratch=[pltpu.VMEM((TAPS * F, 128), F32)],
        name="weights",
    )
    (turned,) = call(
        turn_kernel, (out((STEPS * F, CH), BF),), x, scratch=[pltpu.VMEM((STEPS * F, CH), F32)], name="turn"
    )
    sent = [*sent[:2], *lax.optimization_barrier((turned, w, *sent[2:3]))[2:], *sent[3:]]
    upstream = exchanged(sent)
    u, u_edge = call(
        inner_kernel,
        (out(flat, BF), out((GROWS, CH), BF)),
        halo,
        turned,
        w,
        name="inner",
    )
    before, after = neighbours(u_edge, "fiber")
    slope, *act = call(
        forward_kernel,
        (out(flat, F32),) + (out(chunk, BF),) * n,
        u,
        before,
        after,
        d,
        scratch=[pltpu.VMEM(packed, BF), pltpu.VMEM(flat, F32)],
        name="forward",
    )
    act = exchanged(act)
    dz, dz_edge = call(
        slope_kernel,
        (out(flat, BF), out((GROWS, CH), BF)),
        slope,
        *upstream,
        scratch=[pltpu.VMEM(packed, BF), pltpu.VMEM(flat, F32)],
        name="slope",
    )
    before, after = neighbours(dz_edge, "fiber")
    du, grads, give = call(
        backward_kernel,
        (out(flat, BF), out((F + 8, HALF), F32), out((F + 8, HALF), BF)),
        dz,
        before,
        after,
        dt,
        u,
        halo,
        turned,
        name="backward",
    )
    head = du[0 : LATE * F]
    grads, give, *act = lax.optimization_barrier((grads, give, *act))
    (activation,) = call(
        unpack_kernel, (out((F, local, n * TOUT), BF),), *act, scratch=[pltpu.VMEM(packed, BF)], name="unpack"
    )
    grads = grads + lax.ppermute(give, "rep", CORES).astype(F32)
    hops = [(axis, 1 << k) for axis in ("fiber", "tm") for k in range((lax.axis_size(axis) - 1).bit_length())]
    late = lax.ppermute(head, "tm", [(i + 1, i) for i in range(n - 1)])
    (early,) = call(
        early_kernel,
        (out((F, CH, STEPS), BF),),
        du,
        v,
        scratch=[pltpu.VMEM((STEPS * F, CH), F32)],
        name="early",
    )
    for step, (axis, hop) in enumerate(hops):
        if step == 1:
            grads, activation = lax.optimization_barrier((grads, activation))
        if step == 2:
            grads, early = lax.optimization_barrier((grads, early))
        mine, other = paired(grads, axis, hop)
        grads = mine.astype(F32) + other.astype(F32)
    (strain_grad,) = call(
        signal_kernel,
        (out((F, CH, STEPS), BF),),
        du,
        late,
        v,
        early,
        scratch=[
            pltpu.VMEM(((STEPS - EARLY) * F, CH), F32),
            pltpu.VMEM((F, CH, STEPS), BF),
            pltpu.SemaphoreType.DMA((4,)),
        ],
        name="signal",
        far_outs=(0,),
    )
    grads, strain_grad = lax.optimization_barrier((grads, strain_grad))
    others = lax.ppermute(grads, "rep", CORES)
    time_grad, fiber_grad = call(
        functools.partial(finish_kernel, scale),
        (out((F, F, TAPS), F32), out((KF, PER, F), F32)),
        grads,
        others,
        scratch=[pltpu.VMEM((F * TAPS, 128), F32)],
        name="finish",
    )
    return activation[None, :, None], strain_grad[None], time_grad, jnp.transpose(fiber_grad, (2, 1, 0))


def solution(mesh):
    placed = (
        P(("parts", "rep"), None, "fiber", "tm"),
        P(),
        P(),
        P(("parts", "rep"), None, "fiber", "tm", None),
    )
    return jax.shard_map(
        on_device,
        mesh=mesh,
        in_specs=placed,
        out_specs=(
            P(("parts", "rep"), None, "fiber", "tm", None),
            P(("parts", "rep"), None, "fiber", "tm"),
            P("parts", None, None),
            P("parts", None, None),
        ),
        check_vma=False,
    )
```

```python
import functools
import math

import jax
import jax.numpy as jnp
from jax import lax
from jax.experimental import pallas as pl
from jax.experimental.pallas import tpu as pltpu
from jax.sharding import PartitionSpec as P

F = 32
PER = 4
TAPS = 32
KF = 9
REACH = KF // 2
CH = 128
STEPS = 128
TOUT = STEPS // 2
HALO = 32
TB = 8
WIN = (2 * TB + TAPS) * F
TG = 4
GROWS = TG * F
NG = TOUT // TG
VWIN = 24 * F
CORES = [(0, 1), (1, 0)]
HALF = TAPS * F // 2
EARLY = STEPS - HALO
LATE = 16
BF = jnp.bfloat16
F32 = jnp.float32
NT = (((1,), (1,)), ((), ()))
VMEM_LIMIT = 16 * 1024 * 1024


def call(kernel, outs, *args, scratch=(), name=None, far=(), far_outs=(), same={}):
    where = lambda k, away: pl.BlockSpec(memory_space=pltpu.HBM if k in away else pltpu.VMEM)
    return pl.pallas_call(
        kernel,
        out_shape=outs,
        in_specs=[where(k, far) for k in range(len(args))],
        out_specs=tuple(where(k, far_outs) for k in range(len(outs))),
        scratch_shapes=list(scratch),
        input_output_aliases=same,
        compiler_params=pltpu.CompilerParams(vmem_limit_bytes=VMEM_LIMIT),
        name=name,
    )(*args)


def out(shape, dtype):
    return jax.ShapeDtypeStruct(shape, dtype)


def lanes(shape):
    return lax.broadcasted_iota(jnp.int32, shape, len(shape) - 1)


def rows(shape):
    return lax.broadcasted_iota(jnp.int32, shape, len(shape) - 2)


def roll(x, by, axis=1):
    by = by % x.shape[axis]
    return x if by == 0 else pltpu.roll(x, by, axis)


def place(chunks, refs):
    me = lax.axis_index("tm")
    for hop, ref in enumerate(refs):
        ref[...] = chunks[me ^ hop]


def gather(chunks, refs):
    me = lax.axis_index("tm")
    for hop, ref in enumerate(refs):
        chunks[me ^ hop] = ref[...]


def pack_kernel(cot_ref, *refs):
    chunks = refs[-1]
    n = chunks.shape[0]
    low = lanes((1, 128)) < TOUT
    for f2 in range(F // 2):
        for tile in range(n // 2):
            a = cot_ref[2 * f2, :, 128 * tile : 128 * (tile + 1)]
            b = cot_ref[2 * f2 + 1, :, 128 * tile : 128 * (tile + 1)]
            chunks[2 * tile, f2] = jnp.where(low, a, roll(b, TOUT))
            chunks[2 * tile + 1, f2] = jnp.where(low, roll(a, TOUT), b)
    place(chunks, refs[:-1])


def tail_kernel(strain_ref, halo_out, strain_out, scratch):
    group = lanes((1, 128)) // HALO
    for i4 in range(F // 4):
        tile = roll(strain_ref[4 * i4], HALO)
        for e in range(1, 4):
            tile = jnp.where(group == e, roll(strain_ref[4 * i4 + e], HALO * (e + 1)), tile)
        turned = tile.T.astype(F32)
        for e in range(4):
            scratch[pl.ds(4 * i4 + e, HALO, stride=F), :] = turned[HALO * e : HALO * (e + 1)]
    halo_out[...] = scratch[...].astype(BF)


def turn_kernel(strain_ref, out_ref, scratch):
    for i in range(F):
        scratch[pl.ds(i, STEPS, stride=F), :] = strain_ref[i].T.astype(F32)
    out_ref[...] = scratch[...].astype(BF)


def weight_kernel(time_ref, fiber_ref, w_out, v_out, d_out, dt_out, scratch):
    for o4 in range(F // 4):
        turned = time_ref[4 * o4 : 4 * (o4 + 1)].astype(F32).reshape(4 * F, TAPS)
        turned = jnp.concatenate([turned, jnp.zeros((4 * F, 128 - TAPS), F32)], axis=1).T[0:TAPS]
        for e in range(4):
            scratch[pl.ds(4 * o4 + e, TAPS, stride=F), :] = roll(turned, -F * e)
    group = lanes((1, 128)) // F
    tiles = []
    for k4 in range(TAPS // 4):
        tile = scratch[F * 4 * k4 : F * (4 * k4 + 1)]
        for e in range(1, 4):
            tile = jnp.where(group == e, roll(scratch[F * (4 * k4 + e) : F * (4 * k4 + e + 1)], F * e), tile)
        tiles.append(tile)
    tiles.append(jnp.zeros((F, WIN - TAPS * F), F32))
    base = jnp.concatenate(tiles, axis=1)
    for t in range(TB):
        w_out[F * t : F * (t + 1)] = roll(base, 2 * F * (t + 1)).astype(BF)
    size, step = TB * F, 2 * TB * F
    for a in range(3):
        v_out[:, size * a : size * (a + 1)] = w_out[:, step * (2 - a) : step * (3 - a)].T
    taps = fiber_ref[...]
    spread = (lax.broadcasted_iota(jnp.int32, (F, GROWS), 1) % F == lax.broadcasted_iota(jnp.int32, (F, GROWS), 0)).astype(BF)
    wide = jnp.dot(taps, spread, preferred_element_type=F32).astype(BF)
    row = lax.broadcasted_iota(jnp.int32, (GROWS, GROWS), 0)
    col = lax.broadcasted_iota(jnp.int32, (GROWS, GROWS), 1)
    together = (row // PER) == (col // PER)
    which = lax.broadcasted_iota(jnp.int32, (GROWS, KF * PER), 1)
    feat = lax.broadcasted_iota(jnp.int32, (GROWS, KF * PER), 0) % PER
    for m in range(KF):
        pick = (which == PER * m + feat).astype(BF)
        block = jnp.where(together, jnp.dot(pick, wide, preferred_element_type=F32), 0.0)
        dt_out[:, GROWS * m : GROWS * (m + 1)] = block.astype(BF)
        d_out[:, GROWS * m : GROWS * (m + 1)] = block.T.astype(BF)


def pack_edges(read):
    group = lanes((1, 128)) // 8
    packed = roll(read(0), REACH)
    for g in range(1, NG):
        packed = jnp.where(group == g, roll(read(g), 8 * g + REACH), packed)
    return packed


def edges_of(before_ref, after_ref):
    me, size = lax.axis_index("fiber"), lax.axis_size("fiber")
    first = lanes((1, 128)) % 8 < REACH
    keep_before = jnp.where(me > 0, 1.0, 0.0).astype(F32)
    keep_after = jnp.where(me < size - 1, 1.0, 0.0).astype(F32)
    both = jnp.where(first, before_ref[...].astype(F32) * keep_before, after_ref[...].astype(F32) * keep_after)
    return both.astype(BF)


def shifted_stack(tile, edges, g, shifts):
    around = roll(edges, -(8 * g + REACH))
    lane = lanes((1, 128))
    pieces = []
    for by in shifts:
        if by > 0:
            pieces.append(roll(jnp.where(lane < by, around, tile), -by))
        elif by < 0:
            pieces.append(roll(jnp.where(lane >= CH + by, around, tile), -by))
        else:
            pieces.append(tile)
    return jnp.concatenate(pieces, axis=0)


def window(early_ref, main_ref, b, size):
    start = 2 * TB * F * b
    early = early_ref.shape[0]
    if start >= early:
        return main_ref[start - early : start - early + size]
    return jnp.concatenate([early_ref[start:early], main_ref[0 : size - (early - start)]], axis=0)


def inner_kernel(halo_ref, strain_ref, w_ref, u_out, edge_out):
    size = TB * F
    for b in range(0, TOUT // TB, 2):
        pair = jnp.concatenate([window(halo_ref, strain_ref, b + k, WIN) for k in range(2)], axis=1)
        u = jnp.dot(w_ref[...], pair, preferred_element_type=F32)
        for k in range(2):
            u_out[size * (b + k) : size * (b + k + 1)] = u[:, CH * k : CH * (k + 1)].astype(BF)
    edge_out[...] = pack_edges(lambda g: u_out[GROWS * g : GROWS * (g + 1)])


def forward_kernel(u_ref, before_ref, after_ref, d_ref, slope_out, *refs):
    chunks, scratch = refs[-2:]
    edges = edges_of(before_ref, after_ref)
    for g in range(0, NG, 2):
        pair = jnp.concatenate(
            [
                shifted_stack(
                    u_ref[GROWS * (g + k) : GROWS * (g + k + 1)], edges, g + k, range(-REACH, REACH + 1)
                )
                for k in range(2)
            ],
            axis=1,
        )
        z = jnp.dot(d_ref[...], pair, preferred_element_type=F32).astype(BF).astype(F32)
        half = 0.5 * (1.0 + lax.erf(z * (1.0 / math.sqrt(2.0))))
        slope = half + z * jnp.exp(-0.5 * z * z) * (1.0 / math.sqrt(2.0 * math.pi))
        act = z * half
        for k in range(2):
            where = slice(GROWS * (g + k), GROWS * (g + k + 1))
            scratch[where] = act[:, CH * k : CH * (k + 1)]
            slope_out[where] = slope[:, CH * k : CH * (k + 1)]
    n, _, local, _ = chunks.shape
    for f2 in range(F // 2):
        both = jnp.concatenate([scratch[pl.ds(2 * f2 + e, TOUT, stride=F), :] for e in range(2)], axis=0)
        turned = both.astype(BF).T
        for q in range(n):
            chunks[q, f2] = turned[local * q : local * (q + 1)]
    place(chunks, refs[:-2])


def slope_kernel(slope_ref, *refs):
    dz_out, edge_out, chunks, scratch = refs[-4:]
    gather(chunks, refs[:-4])
    local = chunks.shape[2]
    for f2 in range(F // 2):
        if local % 16 == 0:
            turned = chunks[:, f2].reshape(CH, 128).T.astype(F32)
        else:
            turned = chunks[:, f2].astype(F32).reshape(CH, 128).T
        for e in range(2):
            scratch[pl.ds(2 * f2 + e, TOUT, stride=F), :] = turned[TOUT * e : TOUT * (e + 1)]
    dz_out[...] = (scratch[...] * slope_ref[...]).astype(BF)
    edge_out[...] = pack_edges(lambda g: dz_out[GROWS * g : GROWS * (g + 1)])


def backward_kernel(dz_ref, before_ref, after_ref, dt_ref, u_ref, halo_ref, strain_ref, du_out, keep_out, give_out):
    edges = edges_of(before_ref, after_ref)
    taps = jnp.zeros((GROWS, KF * GROWS), F32)
    for g in range(0, NG, 2):
        stacks = [
            shifted_stack(
                dz_ref[GROWS * (g + k) : GROWS * (g + k + 1)],
                edges,
                g + k,
                [REACH - m for m in range(KF)],
            )
            for k in range(2)
        ]
        pair = jnp.concatenate(stacks, axis=1)
        du = jnp.dot(dt_ref[...], pair, preferred_element_type=F32).astype(BF)
        u = jnp.concatenate([u_ref[GROWS * (g + k) : GROWS * (g + k + 1)] for k in range(2)], axis=1)
        taps = taps + lax.dot_general(u, pair, NT, preferred_element_type=F32)
        for k in range(2):
            du_out[GROWS * (g + k) : GROWS * (g + k + 1)] = du[:, CH * k : CH * (k + 1)]
    lane = lanes((1, KF * GROWS))
    step = (lane % GROWS) // F
    kept = jnp.where(step == 0, taps[0:F], 0.0)
    for t in range(1, TG):
        kept = jnp.where(step == t, taps[F * t : F * (t + 1)], kept)
    feat = lane % F
    row = rows((F, 1))
    lines = []
    for j in range(PER):
        lines.append(jnp.sum(jnp.where(row == feat // PER * PER + j, kept, 0.0), axis=0, keepdims=True))
    lines = jnp.concatenate(lines + [jnp.zeros((8 - PER, KF * GROWS), F32)], axis=0)
    tiles = []
    for top in range(0, KF, TG):
        tile = jnp.zeros((8, GROWS), F32)
        for m in range(top, min(KF, top + TG)):
            line = lines[:, GROWS * m : GROWS * (m + 1)]
            total = line
            for t in range(1, TG):
                total = total + roll(line, F * t)
            tile = jnp.where(lanes((1, GROWS)) // F == m - top, total, tile)
        tiles.append(tile)
    size = TB * F
    wide = jnp.zeros((size, WIN), F32)
    for b in range(0, TOUT // TB, 2):
        left = jnp.concatenate([du_out[size * (b + k) : size * (b + k + 1)] for k in range(2)], axis=1)
        right = jnp.concatenate([window(halo_ref, strain_ref, b + k, WIN) for k in range(2)], axis=1)
        wide = wide + lax.dot_general(left, right, NT, preferred_element_type=F32)
    total = jnp.zeros((F, WIN), F32)
    for t in range(TB):
        total = total + roll(wide[F * t : F * (t + 1)], -2 * F * (t + 1))
    tiles.append(jnp.zeros((8, TAPS * F - len(tiles) * GROWS), F32))
    total = jnp.concatenate([total[:, 0 : TAPS * F], jnp.concatenate(tiles, axis=1)], axis=0)
    lower, upper = total[:, 0:HALF], total[:, HALF : 2 * HALF]
    first = lax.axis_index("rep") == 0
    keep_out[...] = jnp.where(first, lower, upper)
    give_out[...] = jnp.where(first, upper, lower).astype(BF)


def signal_blocks(v_ref, rows_of, blocks, scratch):
    step = 2 * TB * F
    for b in range(0, len(blocks), 2):
        pair = jnp.concatenate([rows_of(blocks[b + k]) for k in range(2)], axis=1)
        part = jnp.dot(v_ref[...], pair, preferred_element_type=F32)
        for k in range(2):
            scratch[step * (b + k) : step * (b + k + 1)] = part[:, CH * k : CH * (k + 1)]


def early_kernel(du_ref, v_ref, early_out, scratch):
    size = TB * F
    scratch[EARLY * F :] = jnp.zeros(((STEPS - EARLY) * F, CH), F32)
    signal_blocks(v_ref, lambda b: du_ref[size * b : size * b + VWIN], range(TOUT // TB - 2), scratch)
    for i in range(F):
        early_out[i] = scratch[pl.ds(i, STEPS, stride=F), :].astype(BF).T


def signal_kernel(du_ref, late_ref, v_ref, early_ref, grad_out, scratch, ready, sems):
    size = TB * F
    last = TOUT * F

    def rows_of(b):
        start, stop = size * b, size * b + VWIN
        return jnp.concatenate([du_ref[start:last], late_ref[0 : stop - last]], axis=0)

    signal_blocks(v_ref, rows_of, range(TOUT // TB - 2, TOUT // TB), scratch)
    count = STEPS - EARLY
    ends = lanes((1, 128)) >= EARLY
    copies = []
    for i4 in range(F // 4):
        four = jnp.concatenate([scratch[pl.ds(4 * i4 + e, count, stride=F), :] for e in range(4)], axis=0)
        turned = four.astype(BF).T
        for e in range(4):
            ready[4 * i4 + e] = jnp.where(ends, roll(turned, EARLY - count * e), early_ref[4 * i4 + e])
        if i4 % 2 == 1:
            part = pl.ds(4 * (i4 - 1), 8)
            copies.append(pltpu.make_async_copy(ready.at[part], grad_out.at[part], sems.at[i4 // 2]))
            copies[-1].start()
    for copy in copies:
        copy.wait()


def unpack_kernel(*refs):
    act_out, chunks = refs[-2:]
    gather(chunks, refs[:-2])
    n = chunks.shape[0]
    low = lanes((1, 128)) < TOUT
    for f2 in range(F // 2):
        for tile in range(n // 2):
            a = chunks[2 * tile, f2]
            b = chunks[2 * tile + 1, f2]
            where = slice(128 * tile, 128 * (tile + 1))
            act_out[2 * f2, :, where] = jnp.where(low, a, roll(b, TOUT))
            act_out[2 * f2 + 1, :, where] = jnp.where(low, roll(a, TOUT), b)


def finish_kernel(scale, mine_ref, other_ref, time_out, fiber_out, scratch):
    first = lax.axis_index("rep") == 0
    mine, other = mine_ref[...], other_ref[...]
    total = jnp.concatenate([jnp.where(first, mine, other), jnp.where(first, other, mine)], axis=1) * scale
    for k in range(TAPS):
        tile = total[0:F, 128 * (k // 4) : 128 * (k // 4 + 1)]
        scratch[pl.ds(k, F, stride=TAPS), :] = roll(tile, -F * (k % 4))
    for o4 in range(F // 4):
        turned = scratch[4 * TAPS * o4 : 4 * TAPS * (o4 + 1)].T[0:F]
        for e in range(4):
            time_out[4 * o4 + e] = roll(turned, -TAPS * e)[:, 0:TAPS]
    for m in range(KF):
        tile = total[F : F + 8, 128 * (m // 4) : 128 * (m // 4 + 1)]
        fiber_out[m] = roll(tile, -F * (m % 4))[0:PER, 0:F]


def exchanged(chunks):
    size = len(chunks)
    got = [chunks[0]]
    for hop in range(1, size):
        got.append(lax.ppermute(chunks[hop], "tm", [(i, i ^ hop) for i in range(size)]))
    return got


def neighbours(array, axis):
    size = lax.axis_size(axis)
    if size == 2:
        other = lax.ppermute(array, axis, [(0, 1), (1, 0)])
        return other, other
    before = lax.ppermute(array, axis, [(i, i + 1) for i in range(size - 1)])
    after = lax.ppermute(array, axis, [(i + 1, i) for i in range(size - 1)])
    return before, after


def paired(array, axis, hop):
    mine = array.astype(BF)
    return mine, lax.ppermute(mine, axis, [(i, i ^ hop) for i in range(lax.axis_size(axis))])


def on_device(strain, time_kernel, fiber_kernel, cotangent):
    n = lax.axis_size("tm")
    size = lax.axis_size("rep") * CH * lax.axis_size("fiber") * TOUT * n
    scale = 1.0 / math.sqrt(size)
    local = cotangent.shape[3]
    x = strain[0]
    chunk = (F // 2, local, 128)
    packed = (n,) + chunk
    flat = (TOUT * F, CH)
    tail, x = call(
        tail_kernel,
        (out((HALO * F, CH), BF), out(x.shape, BF)),
        x,
        scratch=[pltpu.VMEM((HALO * F, CH), F32)],
        name="tail",
        same={0: 1},
    )
    halo = lax.ppermute(tail, "tm", [(i, i + 1) for i in range(n - 1)])
    cot, tail = lax.optimization_barrier((cotangent[0, :, 0], tail))
    sent = call(pack_kernel, (out(chunk, BF),) * n, cot, scratch=[pltpu.VMEM(packed, BF)], name="pack")

    w, v, d, dt = call(
        weight_kernel,
        (
            out((TB * F, WIN), BF),
            out((2 * TB * F, VWIN), BF),
            out((GROWS, KF * GROWS), BF),
            out((GROWS, KF * GROWS), BF),
        ),
        time_kernel,
        jnp.transpose(fiber_kernel, (2, 1, 0)).reshape(KF * PER, F),
        scratch=[pltpu.VMEM((TAPS * F, 128), F32)],
        name="weights",
    )
    (turned,) = call(
        turn_kernel, (out((STEPS * F, CH), BF),), x, scratch=[pltpu.VMEM((STEPS * F, CH), F32)], name="turn"
    )
    sent = [*sent[:2], *lax.optimization_barrier((turned, w, *sent[2:3]))[2:], *sent[3:]]
    upstream = exchanged(sent)
    u, u_edge = call(
        inner_kernel,
        (out(flat, BF), out((GROWS, CH), BF)),
        halo,
        turned,
        w,
        name="inner",
    )
    before, after = neighbours(u_edge, "fiber")
    slope, *act = call(
        forward_kernel,
        (out(flat, F32),) + (out(chunk, BF),) * n,
        u,
        before,
        after,
        d,
        scratch=[pltpu.VMEM(packed, BF), pltpu.VMEM(flat, F32)],
        name="forward",
    )
    act = exchanged(act)
    dz, dz_edge = call(
        slope_kernel,
        (out(flat, BF), out((GROWS, CH), BF)),
        slope,
        *upstream,
        scratch=[pltpu.VMEM(packed, BF), pltpu.VMEM(flat, F32)],
        name="slope",
    )
    before, after = neighbours(dz_edge, "fiber")
    du, grads, give = call(
        backward_kernel,
        (out(flat, BF), out((F + 8, HALF), F32), out((F + 8, HALF), BF)),
        dz,
        before,
        after,
        dt,
        u,
        halo,
        turned,
        name="backward",
    )
    head = du[0 : LATE * F]
    grads, give, *act = lax.optimization_barrier((grads, give, *act))
    (activation,) = call(
        unpack_kernel, (out((F, local, n * TOUT), BF),), *act, scratch=[pltpu.VMEM(packed, BF)], name="unpack"
    )
    grads = grads + lax.ppermute(give, "rep", CORES).astype(F32)
    hops = [(axis, 1 << k) for axis in ("fiber", "tm") for k in range((lax.axis_size(axis) - 1).bit_length())]
    late = lax.ppermute(head, "tm", [(i + 1, i) for i in range(n - 1)])
    (early,) = call(
        early_kernel,
        (out((F, CH, STEPS), BF),),
        du,
        v,
        scratch=[pltpu.VMEM((STEPS * F, CH), F32)],
        name="early",
    )
    for step, (axis, hop) in enumerate(hops):
        if step == 1:
            grads, activation = lax.optimization_barrier((grads, activation))
        if step == 2:
            grads, early = lax.optimization_barrier((grads, early))
        mine, other = paired(grads, axis, hop)
        grads = mine.astype(F32) + other.astype(F32)
    (strain_grad,) = call(
        signal_kernel,
        (out((F, CH, STEPS), BF),),
        du,
        late,
        v,
        early,
        scratch=[
            pltpu.VMEM(((STEPS - EARLY) * F, CH), F32),
            pltpu.VMEM((F, CH, STEPS), BF),
            pltpu.SemaphoreType.DMA((4,)),
        ],
        name="signal",
        far_outs=(0,),
    )
    grads, strain_grad = lax.optimization_barrier((grads, strain_grad))
    others = lax.ppermute(grads, "rep", CORES)
    time_grad, fiber_grad = call(
        functools.partial(finish_kernel, scale),
        (out((F, F, TAPS), F32), out((KF, PER, F), F32)),
        grads,
        others,
        scratch=[pltpu.VMEM((F * TAPS, 128), F32)],
        name="finish",
    )
    return activation[None, :, None], strain_grad[None], time_grad, jnp.transpose(fiber_grad, (2, 1, 0))


def solution(mesh):
    placed = (
        P(("parts", "rep"), None, "fiber", "tm"),
        P(),
        P(),
        P(("parts", "rep"), None, "fiber", "tm", None),
    )
    return jax.shard_map(
        on_device,
        mesh=mesh,
        in_specs=placed,
        out_specs=(
            P(("parts", "rep"), None, "fiber", "tm", None),
            P(("parts", "rep"), None, "fiber", "tm"),
            P("parts", None, None),
            P("parts", None, None),
        ),
        check_vma=False,
    )
```

```python
import functools
import math

import jax
import jax.numpy as jnp
from jax import lax
from jax.experimental import pallas as pl
from jax.experimental.pallas import tpu as pltpu
from jax.sharding import PartitionSpec as P

F = 32
PER = 4
TAPS = 32
KF = 9
REACH = KF // 2
CH = 128
STEPS = 128
TOUT = STEPS // 2
HALO = 32
TB = 8
WIN = (2 * TB + TAPS) * F
TG = 4
GROWS = TG * F
NG = TOUT // TG
VWIN = 24 * F
CORES = [(0, 1), (1, 0)]
HALF = TAPS * F // 2
EARLY = STEPS - HALO
LATE = 16
BF = jnp.bfloat16
F32 = jnp.float32
NT = (((1,), (1,)), ((), ()))
VMEM_LIMIT = 16 * 1024 * 1024


def call(kernel, outs, *args, scratch=(), name=None, far=(), far_outs=(), same={}):
    where = lambda k, away: pl.BlockSpec(memory_space=pltpu.HBM if k in away else pltpu.VMEM)
    return pl.pallas_call(
        kernel,
        out_shape=outs,
        in_specs=[where(k, far) for k in range(len(args))],
        out_specs=tuple(where(k, far_outs) for k in range(len(outs))),
        scratch_shapes=list(scratch),
        input_output_aliases=same,
        compiler_params=pltpu.CompilerParams(vmem_limit_bytes=VMEM_LIMIT),
        name=name,
    )(*args)


def out(shape, dtype):
    return jax.ShapeDtypeStruct(shape, dtype)


def lanes(shape):
    return lax.broadcasted_iota(jnp.int32, shape, len(shape) - 1)


def rows(shape):
    return lax.broadcasted_iota(jnp.int32, shape, len(shape) - 2)


def roll(x, by, axis=1):
    by = by % x.shape[axis]
    return x if by == 0 else pltpu.roll(x, by, axis)


def place(chunks, refs):
    me = lax.axis_index("tm")
    for hop, ref in enumerate(refs):
        ref[...] = chunks[me ^ hop]


def gather(chunks, refs):
    me = lax.axis_index("tm")
    for hop, ref in enumerate(refs):
        chunks[me ^ hop] = ref[...]


def pack_kernel(cot_ref, *refs):
    chunks = refs[-1]
    n = chunks.shape[0]
    low = lanes((1, 128)) < TOUT
    for f2 in range(F // 2):
        for tile in range(n // 2):
            a = cot_ref[2 * f2, :, 128 * tile : 128 * (tile + 1)]
            b = cot_ref[2 * f2 + 1, :, 128 * tile : 128 * (tile + 1)]
            chunks[2 * tile, f2] = jnp.where(low, a, roll(b, TOUT))
            chunks[2 * tile + 1, f2] = jnp.where(low, roll(a, TOUT), b)
    place(chunks, refs[:-1])


def tail_kernel(strain_ref, halo_out, strain_out, scratch):
    group = lanes((1, 128)) // HALO
    for i4 in range(F // 4):
        tile = roll(strain_ref[4 * i4], HALO)
        for e in range(1, 4):
            tile = jnp.where(group == e, roll(strain_ref[4 * i4 + e], HALO * (e + 1)), tile)
        turned = tile.T.astype(F32)
        for e in range(4):
            scratch[pl.ds(4 * i4 + e, HALO, stride=F), :] = turned[HALO * e : HALO * (e + 1)]
    halo_out[...] = scratch[(HALO - TAPS + 2) * F :].astype(BF)


def turn_kernel(strain_ref, out_ref, scratch):
    for i in range(F):
        scratch[pl.ds(i, STEPS, stride=F), :] = strain_ref[i].T.astype(F32)
    out_ref[...] = scratch[...].astype(BF)


def weight_kernel(time_ref, fiber_ref, w_out, v_out, d_out, dt_out, scratch):
    for o4 in range(F // 4):
        turned = time_ref[4 * o4 : 4 * (o4 + 1)].astype(F32).reshape(4 * F, TAPS)
        turned = jnp.concatenate([turned, jnp.zeros((4 * F, 128 - TAPS), F32)], axis=1).T[0:TAPS]
        for e in range(4):
            scratch[pl.ds(4 * o4 + e, TAPS, stride=F), :] = roll(turned, -F * e)
    group = lanes((1, 128)) // F
    tiles = []
    for k4 in range(TAPS // 4):
        tile = scratch[F * 4 * k4 : F * (4 * k4 + 1)]
        for e in range(1, 4):
            tile = jnp.where(group == e, roll(scratch[F * (4 * k4 + e) : F * (4 * k4 + e + 1)], F * e), tile)
        tiles.append(tile)
    tiles.append(jnp.zeros((F, WIN - TAPS * F), F32))
    base = jnp.concatenate(tiles, axis=1)
    for t in range(TB):
        w_out[F * t : F * (t + 1)] = roll(base, 2 * F * (t + 1)).astype(BF)
    size, step = TB * F, 2 * TB * F
    for a in range(3):
        v_out[:, size * a : size * (a + 1)] = w_out[:, step * (2 - a) : step * (3 - a)].T
    taps = fiber_ref[...]
    spread = (lax.broadcasted_iota(jnp.int32, (F, GROWS), 1) % F == lax.broadcasted_iota(jnp.int32, (F, GROWS), 0)).astype(BF)
    wide = jnp.dot(taps, spread, preferred_element_type=F32).astype(BF)
    row = lax.broadcasted_iota(jnp.int32, (GROWS, GROWS), 0)
    col = lax.broadcasted_iota(jnp.int32, (GROWS, GROWS), 1)
    together = (row // PER) == (col // PER)
    which = lax.broadcasted_iota(jnp.int32, (GROWS, KF * PER), 1)
    feat = lax.broadcasted_iota(jnp.int32, (GROWS, KF * PER), 0) % PER
    for m in range(KF):
        pick = (which == PER * m + feat).astype(BF)
        block = jnp.where(together, jnp.dot(pick, wide, preferred_element_type=F32), 0.0)
        dt_out[:, GROWS * m : GROWS * (m + 1)] = block.astype(BF)
        d_out[:, GROWS * m : GROWS * (m + 1)] = block.T.astype(BF)


def pack_edges(read):
    group = lanes((1, 128)) // 8
    packed = roll(read(0), REACH)
    for g in range(1, NG):
        packed = jnp.where(group == g, roll(read(g), 8 * g + REACH), packed)
    return packed


def edges_of(before_ref, after_ref):
    me, size = lax.axis_index("fiber"), lax.axis_size("fiber")
    first = lanes((1, 128)) % 8 < REACH
    keep_before = jnp.where(me > 0, 1.0, 0.0).astype(F32)
    keep_after = jnp.where(me < size - 1, 1.0, 0.0).astype(F32)
    both = jnp.where(first, before_ref[...].astype(F32) * keep_before, after_ref[...].astype(F32) * keep_after)
    return both.astype(BF)


def shifted_stack(tile, edges, g, shifts):
    around = roll(edges, -(8 * g + REACH))
    lane = lanes((1, 128))
    pieces = []
    for by in shifts:
        if by > 0:
            pieces.append(roll(jnp.where(lane < by, around, tile), -by))
        elif by < 0:
            pieces.append(roll(jnp.where(lane >= CH + by, around, tile), -by))
        else:
            pieces.append(tile)
    return jnp.concatenate(pieces, axis=0)


def window(early_ref, main_ref, b, size):
    start, early = 2 * TB * F * b, HALO * F
    if start >= early:
        return main_ref[start - early : start - early + size]
    unused = early - early_ref.shape[0]
    pieces = [main_ref[start:unused]] if start < unused else []
    pieces += [early_ref[max(start - unused, 0) :], main_ref[0 : size - (early - start)]]
    return jnp.concatenate(pieces, axis=0)


def inner_kernel(halo_ref, strain_ref, w_ref, u_out, edge_out):
    size = TB * F
    for b in range(0, TOUT // TB, 2):
        pair = jnp.concatenate([window(halo_ref, strain_ref, b + k, WIN) for k in range(2)], axis=1)
        u = jnp.dot(w_ref[...], pair, preferred_element_type=F32)
        for k in range(2):
            u_out[size * (b + k) : size * (b + k + 1)] = u[:, CH * k : CH * (k + 1)].astype(BF)
    edge_out[...] = pack_edges(lambda g: u_out[GROWS * g : GROWS * (g + 1)])


def forward_kernel(u_ref, before_ref, after_ref, d_ref, slope_out, *refs):
    chunks, scratch = refs[-2:]
    edges = edges_of(before_ref, after_ref)
    for g in range(0, NG, 2):
        pair = jnp.concatenate(
            [
                shifted_stack(
                    u_ref[GROWS * (g + k) : GROWS * (g + k + 1)], edges, g + k, range(-REACH, REACH + 1)
                )
                for k in range(2)
            ],
            axis=1,
        )
        z = jnp.dot(d_ref[...], pair, preferred_element_type=F32).astype(BF).astype(F32)
        half = 0.5 * (1.0 + lax.erf(z * (1.0 / math.sqrt(2.0))))
        slope = half + z * jnp.exp(-0.5 * z * z) * (1.0 / math.sqrt(2.0 * math.pi))
        act = z * half
        for k in range(2):
            where = slice(GROWS * (g + k), GROWS * (g + k + 1))
            scratch[where] = act[:, CH * k : CH * (k + 1)]
            slope_out[where] = slope[:, CH * k : CH * (k + 1)]
    n, _, local, _ = chunks.shape
    for f2 in range(F // 2):
        both = jnp.concatenate([scratch[pl.ds(2 * f2 + e, TOUT, stride=F), :] for e in range(2)], axis=0)
        turned = both.astype(BF).T
        for q in range(n):
            chunks[q, f2] = turned[local * q : local * (q + 1)]
    place(chunks, refs[:-2])


def slope_kernel(slope_ref, *refs):
    dz_out, edge_out, chunks, scratch = refs[-4:]
    gather(chunks, refs[:-4])
    local = chunks.shape[2]
    for f2 in range(F // 2):
        if local % 16 == 0:
            turned = chunks[:, f2].reshape(CH, 128).T.astype(F32)
        else:
            turned = chunks[:, f2].astype(F32).reshape(CH, 128).T
        for e in range(2):
            scratch[pl.ds(2 * f2 + e, TOUT, stride=F), :] = turned[TOUT * e : TOUT * (e + 1)]
    dz_out[...] = (scratch[...] * slope_ref[...]).astype(BF)
    edge_out[...] = pack_edges(lambda g: dz_out[GROWS * g : GROWS * (g + 1)])


def backward_kernel(dz_ref, before_ref, after_ref, dt_ref, u_ref, halo_ref, strain_ref, du_out, keep_out, give_out):
    edges = edges_of(before_ref, after_ref)
    taps = jnp.zeros((GROWS, KF * GROWS), F32)
    for g in range(0, NG, 2):
        stacks = [
            shifted_stack(
                dz_ref[GROWS * (g + k) : GROWS * (g + k + 1)],
                edges,
                g + k,
                [REACH - m for m in range(KF)],
            )
            for k in range(2)
        ]
        pair = jnp.concatenate(stacks, axis=1)
        du = jnp.dot(dt_ref[...], pair, preferred_element_type=F32).astype(BF)
        u = jnp.concatenate([u_ref[GROWS * (g + k) : GROWS * (g + k + 1)] for k in range(2)], axis=1)
        taps = taps + lax.dot_general(u, pair, NT, preferred_element_type=F32)
        for k in range(2):
            du_out[GROWS * (g + k) : GROWS * (g + k + 1)] = du[:, CH * k : CH * (k + 1)]
    lane = lanes((1, KF * GROWS))
    step = (lane % GROWS) // F
    kept = jnp.where(step == 0, taps[0:F], 0.0)
    for t in range(1, TG):
        kept = jnp.where(step == t, taps[F * t : F * (t + 1)], kept)
    feat = lane % F
    row = rows((F, 1))
    lines = []
    for j in range(PER):
        lines.append(jnp.sum(jnp.where(row == feat // PER * PER + j, kept, 0.0), axis=0, keepdims=True))
    lines = jnp.concatenate(lines + [jnp.zeros((8 - PER, KF * GROWS), F32)], axis=0)
    tiles = []
    for top in range(0, KF, TG):
        tile = jnp.zeros((8, GROWS), F32)
        for m in range(top, min(KF, top + TG)):
            line = lines[:, GROWS * m : GROWS * (m + 1)]
            total = line
            for t in range(1, TG):
                total = total + roll(line, F * t)
            tile = jnp.where(lanes((1, GROWS)) // F == m - top, total, tile)
        tiles.append(tile)
    size = TB * F
    wide = jnp.zeros((size, WIN), F32)
    for b in range(0, TOUT // TB, 2):
        left = jnp.concatenate([du_out[size * (b + k) : size * (b + k + 1)] for k in range(2)], axis=1)
        right = jnp.concatenate([window(halo_ref, strain_ref, b + k, WIN) for k in range(2)], axis=1)
        wide = wide + lax.dot_general(left, right, NT, preferred_element_type=F32)
    total = jnp.zeros((F, WIN), F32)
    for t in range(TB):
        total = total + roll(wide[F * t : F * (t + 1)], -2 * F * (t + 1))
    tiles.append(jnp.zeros((8, TAPS * F - len(tiles) * GROWS), F32))
    total = jnp.concatenate([total[:, 0 : TAPS * F], jnp.concatenate(tiles, axis=1)], axis=0)
    lower, upper = total[:, 0:HALF], total[:, HALF : 2 * HALF]
    first = lax.axis_index("rep") == 0
    keep_out[...] = jnp.where(first, lower, upper)
    give_out[...] = jnp.where(first, upper, lower).astype(BF)


def signal_blocks(v_ref, rows_of, blocks, scratch):
    step = 2 * TB * F
    for b in range(0, len(blocks), 2):
        pair = jnp.concatenate([rows_of(blocks[b + k]) for k in range(2)], axis=1)
        part = jnp.dot(v_ref[...], pair, preferred_element_type=F32)
        for k in range(2):
            scratch[step * (b + k) : step * (b + k + 1)] = part[:, CH * k : CH * (k + 1)]


def early_kernel(du_ref, v_ref, early_out, scratch):
    size = TB * F
    scratch[EARLY * F :] = jnp.zeros(((STEPS - EARLY) * F, CH), F32)
    signal_blocks(v_ref, lambda b: du_ref[size * b : size * b + VWIN], range(TOUT // TB - 2), scratch)
    for i in range(F):
        early_out[i] = scratch[pl.ds(i, STEPS, stride=F), :].astype(BF).T


def signal_kernel(du_ref, late_ref, v_ref, early_ref, grad_out, scratch, ready, sems):
    size = TB * F
    last = TOUT * F

    def rows_of(b):
        start, stop = size * b, size * b + VWIN
        return jnp.concatenate([du_ref[start:last], late_ref[0 : stop - last]], axis=0)

    signal_blocks(v_ref, rows_of, range(TOUT // TB - 2, TOUT // TB), scratch)
    count = STEPS - EARLY
    ends = lanes((1, 128)) >= EARLY
    copies = []
    for i4 in range(F // 4):
        four = jnp.concatenate([scratch[pl.ds(4 * i4 + e, count, stride=F), :] for e in range(4)], axis=0)
        turned = four.astype(BF).T
        for e in range(4):
            ready[4 * i4 + e] = jnp.where(ends, roll(turned, EARLY - count * e), early_ref[4 * i4 + e])
        if i4 % 2 == 1:
            part = pl.ds(4 * (i4 - 1), 8)
            copies.append(pltpu.make_async_copy(ready.at[part], grad_out.at[part], sems.at[i4 // 2]))
            copies[-1].start()
    for copy in copies:
        copy.wait()


def unpack_kernel(*refs):
    act_out, chunks = refs[-2:]
    gather(chunks, refs[:-2])
    n = chunks.shape[0]
    low = lanes((1, 128)) < TOUT
    for f2 in range(F // 2):
        for tile in range(n // 2):
            a = chunks[2 * tile, f2]
            b = chunks[2 * tile + 1, f2]
            where = slice(128 * tile, 128 * (tile + 1))
            act_out[2 * f2, :, where] = jnp.where(low, a, roll(b, TOUT))
            act_out[2 * f2 + 1, :, where] = jnp.where(low, roll(a, TOUT), b)


def finish_kernel(scale, mine_ref, other_ref, time_out, fiber_out, scratch):
    first = lax.axis_index("rep") == 0
    mine, other = mine_ref[...], other_ref[...]
    total = jnp.concatenate([jnp.where(first, mine, other), jnp.where(first, other, mine)], axis=1) * scale
    for k in range(TAPS):
        tile = total[0:F, 128 * (k // 4) : 128 * (k // 4 + 1)]
        scratch[pl.ds(k, F, stride=TAPS), :] = roll(tile, -F * (k % 4))
    for o4 in range(F // 4):
        turned = scratch[4 * TAPS * o4 : 4 * TAPS * (o4 + 1)].T[0:F]
        for e in range(4):
            time_out[4 * o4 + e] = roll(turned, -TAPS * e)[:, 0:TAPS]
    for m in range(KF):
        tile = total[F : F + 8, 128 * (m // 4) : 128 * (m // 4 + 1)]
        fiber_out[m] = roll(tile, -F * (m % 4))[0:PER, 0:F]


def exchanged(chunks):
    size = len(chunks)
    got = [chunks[0]]
    for hop in range(1, size):
        got.append(lax.ppermute(chunks[hop], "tm", [(i, i ^ hop) for i in range(size)]))
    return got


def neighbours(array, axis):
    size = lax.axis_size(axis)
    if size == 2:
        other = lax.ppermute(array, axis, [(0, 1), (1, 0)])
        return other, other
    before = lax.ppermute(array, axis, [(i, i + 1) for i in range(size - 1)])
    after = lax.ppermute(array, axis, [(i + 1, i) for i in range(size - 1)])
    return before, after


def paired(array, axis, hop):
    mine = array.astype(BF)
    return mine, lax.ppermute(mine, axis, [(i, i ^ hop) for i in range(lax.axis_size(axis))])


def on_device(strain, time_kernel, fiber_kernel, cotangent):
    n = lax.axis_size("tm")
    size = lax.axis_size("rep") * CH * lax.axis_size("fiber") * TOUT * n
    scale = 1.0 / math.sqrt(size)
    local = cotangent.shape[3]
    x = strain[0]
    chunk = (F // 2, local, 128)
    packed = (n,) + chunk
    flat = (TOUT * F, CH)
    tail, x = call(
        tail_kernel,
        (out(((TAPS - 2) * F, CH), BF), out(x.shape, BF)),
        x,
        scratch=[pltpu.VMEM((HALO * F, CH), F32)],
        name="tail",
        same={0: 1},
    )
    halo = lax.ppermute(tail, "tm", [(i, i + 1) for i in range(n - 1)])
    cot, tail = lax.optimization_barrier((cotangent[0, :, 0], tail))
    sent = call(pack_kernel, (out(chunk, BF),) * n, cot, scratch=[pltpu.VMEM(packed, BF)], name="pack")

    w, v, d, dt = call(
        weight_kernel,
        (
            out((TB * F, WIN), BF),
            out((2 * TB * F, VWIN), BF),
            out((GROWS, KF * GROWS), BF),
            out((GROWS, KF * GROWS), BF),
        ),
        time_kernel,
        jnp.transpose(fiber_kernel, (2, 1, 0)).reshape(KF * PER, F),
        scratch=[pltpu.VMEM((TAPS * F, 128), F32)],
        name="weights",
    )
    (turned,) = call(
        turn_kernel, (out((STEPS * F, CH), BF),), x, scratch=[pltpu.VMEM((STEPS * F, CH), F32)], name="turn"
    )
    sent = [*sent[:2], *lax.optimization_barrier((turned, w, *sent[2:3]))[2:], *sent[3:]]
    upstream = exchanged(sent)
    u, u_edge = call(
        inner_kernel,
        (out(flat, BF), out((GROWS, CH), BF)),
        halo,
        turned,
        w,
        name="inner",
    )
    before, after = neighbours(u_edge, "fiber")
    slope, *act = call(
        forward_kernel,
        (out(flat, F32),) + (out(chunk, BF),) * n,
        u,
        before,
        after,
        d,
        scratch=[pltpu.VMEM(packed, BF), pltpu.VMEM(flat, F32)],
        name="forward",
    )
    act = exchanged(act)
    dz, dz_edge = call(
        slope_kernel,
        (out(flat, BF), out((GROWS, CH), BF)),
        slope,
        *upstream,
        scratch=[pltpu.VMEM(packed, BF), pltpu.VMEM(flat, F32)],
        name="slope",
    )
    before, after = neighbours(dz_edge, "fiber")
    du, grads, give = call(
        backward_kernel,
        (out(flat, BF), out((F + 8, HALF), F32), out((F + 8, HALF), BF)),
        dz,
        before,
        after,
        dt,
        u,
        halo,
        turned,
        name="backward",
    )
    head = du[0 : LATE * F]
    grads, give, *act = lax.optimization_barrier((grads, give, *act))
    (activation,) = call(
        unpack_kernel, (out((F, local, n * TOUT), BF),), *act, scratch=[pltpu.VMEM(packed, BF)], name="unpack"
    )
    grads = grads + lax.ppermute(give, "rep", CORES).astype(F32)
    hops = [(axis, 1 << k) for axis in ("fiber", "tm") for k in range((lax.axis_size(axis) - 1).bit_length())]
    late = lax.ppermute(head, "tm", [(i + 1, i) for i in range(n - 1)])
    (early,) = call(
        early_kernel,
        (out((F, CH, STEPS), BF),),
        du,
        v,
        scratch=[pltpu.VMEM((STEPS * F, CH), F32)],
        name="early",
    )
    for step, (axis, hop) in enumerate(hops):
        if step == 1:
            grads, early = lax.optimization_barrier((grads, early))
        if step == 2:
            grads, activation = lax.optimization_barrier((grads, activation))
        mine, other = paired(grads, axis, hop)
        grads = mine.astype(F32) + other.astype(F32)
    (strain_grad,) = call(
        signal_kernel,
        (out((F, CH, STEPS), BF),),
        du,
        late,
        v,
        early,
        scratch=[
            pltpu.VMEM(((STEPS - EARLY) * F, CH), F32),
            pltpu.VMEM((F, CH, STEPS), BF),
            pltpu.SemaphoreType.DMA((4,)),
        ],
        name="signal",
        far_outs=(0,),
    )
    grads, strain_grad = lax.optimization_barrier((grads, strain_grad))
    others = lax.ppermute(grads, "rep", CORES)
    time_grad, fiber_grad = call(
        functools.partial(finish_kernel, scale),
        (out((F, F, TAPS), F32), out((KF, PER, F), F32)),
        grads,
        others,
        scratch=[pltpu.VMEM((F * TAPS, 128), F32)],
        name="finish",
    )
    return activation[None, :, None], strain_grad[None], time_grad, jnp.transpose(fiber_grad, (2, 1, 0))


def solution(mesh):
    placed = (
        P(("parts", "rep"), None, "fiber", "tm"),
        P(),
        P(),
        P(("parts", "rep"), None, "fiber", "tm", None),
    )
    return jax.shard_map(
        on_device,
        mesh=mesh,
        in_specs=placed,
        out_specs=(
            P(("parts", "rep"), None, "fiber", "tm", None),
            P(("parts", "rep"), None, "fiber", "tm"),
            P("parts", None, None),
            P("parts", None, None),
        ),
        check_vma=False,
    )
```
